32 devices in a mesh: gx: 8 (over y, x, core), gy: 4 (over z).
Axes of the slice: x: 2, y: 2, z: 4, core: 2. Of those that a mesh axis runs over, the one named last changes fastest.
Arguments:
- prior_fields: bfloat16 [512, 16, 1024], P('gx', 'gy'), may hold values from -17 to 17
- measured_spread: bfloat16 [512, 4, 1024], P(None, 'gy', 'gx'), may hold values from -10 to 10
- scaled_misfit: bfloat16 [4, 1024], P('gy', 'gx'), may hold values from -12 to 12
- sensor_line_inside: int32 [4, 1024], P('gy', 'gx'), may hold values from 0 to 3
Outputs:
- analysis: bfloat16 [512, 16, 1024], P(None, 'gy', 'gx')
The draws below stay inside these ranges and needn't reach their ends.
All inputs are finite; a program needn't handle non-finite values. Where the reference program divides by a largest or mean magnitude, that divisor is 1e-20 or more.
Results may differ from the reference program's by a relative error of at most 0.0053.
Values may be sent and summed in bfloat16 or wider, within the bound.
No kernel may reach another device: no remote copies, remote signals or barrier semaphores. Data moves between devices by JAX's collectives and lax.ppermute only.
A program may use at most 64 MiB of HBM per device.

```python
import jax
import jax.numpy as jnp
from jax import lax

K = 512
BLOCK_WIDTH_X = 128
CY = 4
OY = 1
OX = 128
CP = 2
NEWTON = 2
NY = 16
NX = 1024
NOY = 4
NOX = 1024
N_GX = 8
N_GY = 4


def member_loadings(base_key, mode_count):
    sign_key, size_key = jax.random.split(jax.random.fold_in(base_key, 101))
    sign_values = jax.random.rademacher(sign_key, (K, mode_count), dtype=jnp.float32)
    magnitude = jax.random.uniform(size_key, (K, mode_count), jnp.float32, 0.6, 1.4)
    return sign_values * magnitude


def mode_sum(base_key, salt_value, cell_count, leading, slope, noise_scale, limit_value, levels):
    mode_count = max(4, K // 4)
    loadings = member_loadings(base_key, mode_count)
    field_key, noise_key = jax.random.split(jax.random.fold_in(base_key, salt_value))
    mode_order = jnp.arange(1, mode_count + 1, dtype=jnp.float32)
    strengths = leading * mode_order ** (-slope)
    fields = jax.random.truncated_normal(field_key, -4.0, 4.0, (mode_count, cell_count), jnp.float32)
    noise_part = noise_scale * jax.random.truncated_normal(noise_key, -4.0, 4.0, (K, cell_count), jnp.float32)
    mode_part = jnp.dot(loadings * strengths[None, :], fields, precision=lax.Precision.HIGHEST)
    return jnp.clip((mode_part + noise_part) * levels[None, :], -limit_value, limit_value)


def draw_prior_fields(key, part):
    cell_count = NY * NX
    levels = jnp.ones((cell_count,), jnp.float32)
    member_part = mode_sum(key, 202, cell_count, 1.0, 0.5, 0.5, 16.0, levels)
    mean_key = jax.random.fold_in(key, 303)
    mean_field = 0.2 * jax.random.truncated_normal(mean_key, -4.0, 4.0, (cell_count,), jnp.float32)
    return (member_part + mean_field[None, :]).reshape(K, NY, NX).astype(jnp.bfloat16)


def draw_measured_spread(key, part):
    cell_count = NOY * NOX
    level_key = jax.random.fold_in(key, 505)
    tile_levels = jnp.exp(jax.random.uniform(level_key, (NOY, NOX // OX), jnp.float32, -1.2, 1.2))
    levels = jnp.repeat(tile_levels, OX, axis=1).reshape(-1)
    return mode_sum(key, 404, cell_count, 0.045, 0.15, 0.3, 10.0, levels).reshape(K, NOY, NOX).astype(jnp.bfloat16)


def touch_ends(array, stream_key, low, high):
    longest = array.shape.index(max(array.shape))
    spots = []
    for shift in (0, 1):
        where = [jax.random.randint(jax.random.fold_in(stream_key, axis), (), 0, length) for axis, length in enumerate(array.shape)]
        where[longest] = (where[longest] + shift) % array.shape[longest]
        spots.append(tuple(where))
    return array.at[spots[0]].set(low).at[spots[1]].set(high)


def block_levels(own_key, dims, cuts, low, high):
    factor_of = 1.0
    for dim, shards_of in cuts:
        heights = jax.random.uniform(jax.random.fold_in(jax.random.fold_in(own_key, 6), dim), (shards_of,), jnp.float32, low / len(cuts), high / len(cuts))
        factor_of = factor_of * jnp.repeat(jnp.exp(heights), dims[dim] // shards_of).reshape((-1,) + (1,) * (len(dims) - 1 - dim))
    return factor_of


def gaussian(stream_key, extent, scale, bound, cuts=(), kind=jnp.bfloat16):
    values = scale * jax.random.normal(stream_key, extent, jnp.float32)
    if cuts:
        values = values * block_levels(stream_key, extent, cuts, -0.22, 0.18)
    return jnp.clip(values, -bound, bound).astype(kind)


def setup_inputs(seed: int = 0) -> dict:
    splits = jax.random.split(jax.random.key(seed), 5)
    return {
        "prior_fields": draw_prior_fields(jax.random.fold_in(splits[4], 71), 0),
        "measured_spread": draw_measured_spread(jax.random.fold_in(splits[4], 71), 0),
        "scaled_misfit": gaussian(splits[2], (NOY, NOX), 2.0, 12.0, ((0, 4), (1, 8))),
        "sensor_line_inside": touch_ends(jax.random.randint(splits[3], (NOY, NOX), 0, CY), jax.random.fold_in(splits[3], 1), 0, CY - 1).astype(jnp.int32),
    }


highest = lax.Precision.HIGHEST

def localize(positions, centre, radius):
    distance = (positions - centre) / radius
    return jnp.exp(-0.5 * distance * distance)

def newton_weights(gram_matrix, drive_vector, sweeps):
    sample_count = gram_matrix.shape[0]
    identity = jnp.eye(sample_count, dtype=jnp.float32)
    scaled_gram = identity + gram_matrix / (sample_count - 1.0)
    row_bound = jnp.max(lax.optimization_barrier(jnp.sum(jnp.abs(scaled_gram), axis=1)))
    iterate = scaled_gram / row_bound
    inverse = identity
    for newton_step in range(sweeps):
        if newton_step == 0:
            factor = 0.5 * (3.0 * identity - iterate)
            inverse = factor
        else:
            factor = 0.5 * (3.0 * identity - jnp.dot(inverse, iterate, precision=highest))
            inverse = jnp.dot(factor, inverse, precision=highest)
        if newton_step + 1 < sweeps:
            iterate = jnp.dot(iterate, factor, precision=highest)
    first_pass = jnp.dot(inverse, drive_vector, precision=highest)
    mean_weights = jnp.dot(inverse, first_pass, precision=highest) / (row_bound * (sample_count - 1.0))
    return (inverse / jnp.sqrt(row_bound) + mean_weights[:, None]).astype(jnp.bfloat16)

def coarse_weights(obs_block, innov_block, positions, centre, radius):
    locality = localize(positions, centre, radius)
    scaled = (obs_block.astype(jnp.float32) * locality[None, :]).astype(jnp.bfloat16)
    gram_matrix = lax.dot_general(scaled, obs_block, (((1,), (1,)), ((), ())), preferred_element_type=jnp.float32)
    drive_vector = jnp.dot(scaled, innov_block, preferred_element_type=jnp.float32)
    return newton_weights(gram_matrix, drive_vector, NEWTON)

def hat_weights(row_centres, centre, spacing, height):
    clipped = jnp.clip(row_centres, 0.5 * spacing, height - 0.5 * spacing)
    return jnp.maximum(0.0, 1.0 - jnp.abs(clipped - centre) / spacing)

def apply_weights(transform, state_block, interp):
    sample_count, row_count, cell_count = state_block.shape
    product = lax.dot_general(transform, state_block.reshape(sample_count, row_count * cell_count), (((0,), (0,)), ((), ())), preferred_element_type=jnp.float32)
    return product.reshape(sample_count, row_count, cell_count) * interp[None, :, None]

def reference(prior_fields, measured_spread, scaled_misfit, sensor_line_inside):
    sample_count = prior_fields.shape[0]
    spacing = CY // CP
    point_count = CP * N_GY
    window = 2 * spacing
    pert_tiles = jnp.pad(measured_spread.reshape(sample_count, N_GY, OY, N_GX, OX), ((0, 0), (1, 1), (0, 0), (0, 0), (0, 0)))
    innov_tiles = jnp.pad(scaled_misfit.reshape(N_GY, OY, N_GX, OX), ((1, 1), (0, 0), (0, 0), (0, 0)))
    row_tiles = jnp.pad(sensor_line_inside.reshape(N_GY, OY, N_GX, OX), ((1, 1), (0, 0), (0, 0), (0, 0)))
    tile_base = (jnp.arange(N_GY + 2, dtype=jnp.int32) - 1) * CY
    pos_tiles = (tile_base[:, None, None, None] + row_tiles).astype(jnp.float32) + 0.5

    def one_column(block_for_lane):
        pert_column = lax.dynamic_index_in_dim(pert_tiles, block_for_lane, 3, keepdims=False)
        innov_column = lax.dynamic_index_in_dim(innov_tiles, block_for_lane, 2, keepdims=False)
        pos_column = lax.dynamic_index_in_dim(pos_tiles, block_for_lane, 2, keepdims=False)

        def one_point(point_index):
            row_tile = point_index // CP
            obs_block = lax.dynamic_slice_in_dim(pert_column, row_tile, 3, 1).reshape(sample_count, -1)
            innov_block = lax.dynamic_slice_in_dim(innov_column, row_tile, 3, 0).reshape(-1)
            positions = lax.dynamic_slice_in_dim(pos_column, row_tile, 3, 0).reshape(-1)
            centre = (point_index.astype(jnp.float32) + 0.5) * spacing
            return coarse_weights(obs_block, innov_block, positions, centre, float(CY))
        all_weights = lax.map(one_point, jnp.arange(point_count, dtype=jnp.int32))
        prior_by_lane = lax.dynamic_slice_in_dim(prior_fields, block_for_lane * BLOCK_WIDTH_X, BLOCK_WIDTH_X, 2)
        state_mean = lax.optimization_barrier(jnp.sum(prior_by_lane, axis=0, dtype=jnp.float32)) / sample_count
        deviation = (prior_by_lane.astype(jnp.float32) - state_mean[None]).astype(jnp.bfloat16)

        def add_point(increment, point_index):
            first_row = jnp.clip(point_index * spacing - spacing // 2, 0, NY - window)
            state_block = lax.dynamic_slice_in_dim(deviation, first_row, window, 1)
            row_centres = (first_row + jnp.arange(window, dtype=jnp.int32)).astype(jnp.float32) + 0.5
            centre = (point_index.astype(jnp.float32) + 0.5) * spacing
            interp = hat_weights(row_centres, centre, spacing, NY)
            term_block = apply_weights(all_weights[point_index], state_block, interp)
            current = lax.dynamic_slice_in_dim(increment, first_row, window, 1)
            return (lax.dynamic_update_slice_in_dim(increment, current + term_block, first_row, 1), None)
        increment, unused = lax.scan(add_point, jnp.zeros(deviation.shape, jnp.float32), jnp.arange(point_count, dtype=jnp.int32))
        return (state_mean[None] + increment).astype(jnp.bfloat16)
    columns = lax.map(one_column, jnp.arange(N_GX, dtype=jnp.int32))
    return jnp.transpose(columns, (1, 2, 0, 3)).reshape(sample_count, NY, N_GX * BLOCK_WIDTH_X)
```

```python
import functools

import jax
import jax.numpy as jnp
from jax import lax
from jax.experimental import pallas as pl
from jax.experimental.pallas import tpu as pltpu
from jax.sharding import PartitionSpec as P

CP = 2
PAD = 16
MIB = 1 << 20

VMEM = pl.BlockSpec(memory_space=pltpu.VMEM)


def swap_pairs(size, reach, phase):
    lows = [i for i in range(size - reach) if (i // reach) % 2 == phase]
    return [pair for i in lows for pair in ((i, i + reach), (i + reach, i))]


def prepare_kernel(parts, rows, prior_ref, spread_ref, misfit_ref, line_ref, packed_ref, sorted_ref, wide):
    members = prior_ref.shape[0] // (parts * rows)
    count = spread_ref.shape[0]
    packed_ref[0:count, :] = spread_ref[...]
    width = spread_ref.shape[1]
    which = lax.broadcasted_iota(jnp.int32, (PAD, width), 0)
    misfit = jnp.broadcast_to(misfit_ref[...].astype(jnp.float32), (PAD, width))
    line = jnp.broadcast_to(line_ref[...].astype(jnp.float32), (PAD, width))
    extra = jnp.where(which == 0, misfit, jnp.where(which == 1, line, 0.0))
    packed_ref[count:, :] = extra.astype(jnp.bfloat16)
    wide[...] = prior_ref[...].astype(jnp.float32)
    for part in range(parts):
        for row in range(rows):
            lines = wide[pl.ds(part * rows + row, members, stride=parts * rows), :]
            sorted_ref[part, row] = lines.astype(jnp.bfloat16)


def prepare(prior, spread, misfit, line, parts):
    members, rows, cells = prior.shape
    width = cells // parts
    count, obs = spread.shape
    flat = prior.reshape(members, rows, parts, width).transpose(0, 2, 1, 3).reshape(-1, width)
    return pl.pallas_call(
        functools.partial(prepare_kernel, parts, rows),
        out_shape=(
            jax.ShapeDtypeStruct((count + PAD, obs), jnp.bfloat16),
            jax.ShapeDtypeStruct((parts, rows, members, width), jnp.bfloat16),
        ),
        in_specs=[VMEM] * 4,
        out_specs=(VMEM, VMEM),
        scratch_shapes=[pltpu.VMEM(flat.shape, jnp.float32)],
        compiler_params=pltpu.CompilerParams(vmem_limit_bytes=24 * MIB),
        name="prepare",
    )(flat, spread, misfit, line)


def select_flag(condition):
    return jnp.where(condition, jnp.float32(1.0), jnp.float32(0.0))


def point_weights(left, count, radius, centre, bases, present):
    line = left[count + 1 : count + 2, :].astype(jnp.float32)
    obs = line.shape[1] // 3
    where = lax.broadcasted_iota(jnp.int32, line.shape, 1) // obs
    base = jnp.where(where == 0, bases[0], jnp.where(where == 1, bases[1], bases[2]))
    alive = jnp.where(where == 0, present[0], jnp.where(where == 1, present[1], present[2]))
    distance = (base + line + 0.5 - centre) / radius
    locality = jnp.exp(-0.5 * distance * distance) * alive
    scaled = (left[0:count, :].astype(jnp.float32) * locality).astype(jnp.bfloat16)
    both = lax.dot_general(
        left[...], scaled, (((1,), (1,)), ((), ())), preferred_element_type=jnp.float32
    )
    gram = both[0:count]
    drive = both[count : count + 1]
    share = 1.0 / (count - 1.0)
    on_diagonal = lax.broadcasted_iota(jnp.int32, gram.shape, 0) == lax.broadcasted_iota(
        jnp.int32, gram.shape, 1
    )
    sizes = jnp.abs(jnp.where(on_diagonal, 1.0, 0.0) + gram * share)
    bound = jnp.max(jnp.sum(sizes, axis=0, keepdims=True), axis=1, keepdims=True)
    rounded = gram.astype(jnp.bfloat16)
    square = jnp.dot(rounded, rounded, preferred_element_type=jnp.float32)
    s = 1.0 / bound
    g = s * share
    first = jnp.broadcast_to(g, (1, count))
    second = jnp.broadcast_to(g * g, (1, count))
    beta = s * s - 9.0 * s
    quad = second * square
    x = (2.0 * s) * first * gram + quad
    w = (2.0 * s - 9.0) * first * gram + quad
    product = jnp.dot(x.astype(jnp.bfloat16), w.astype(jnp.bfloat16), preferred_element_type=jnp.float32)
    on_gram = (-39.0 + (27.0 + beta) * (2.0 * s) + s * s * (2.0 * s - 9.0)) * first / 16.0
    on_square = (27.0 + beta + s * s) * second / 16.0
    rest = on_gram * gram + on_square * square + product * (1.0 / 16.0)
    scalar_part = (36.0 + s * (-39.0 + s * (27.0 + s * (-9.0 + s)))) / 16.0
    rest_rounded = rest.astype(jnp.bfloat16)

    def row_times(row):
        high = row.astype(jnp.bfloat16).astype(jnp.float32)
        which = lax.broadcasted_iota(jnp.int32, (PAD, count), 0)
        two = jnp.where(which == 0, high, jnp.where(which == 1, row - high, 0.0))
        out = jnp.dot(two.astype(jnp.bfloat16), rest_rounded, preferred_element_type=jnp.float32)
        return out[0:1] + out[1:2] + scalar_part * row

    mean_weights = row_times(row_times(drive)) * g
    root = lax.rsqrt(bound)
    return rest * jnp.broadcast_to(root, (1, count)), scalar_part * root, mean_weights


def weights_kernel(size, rows, spacing, has_far, *refs):
    own_ref, first_ref, other_ref = refs[:3]
    far_refs = refs[3 : 3 + sum(has_far)]
    mix_ref, diag_ref, left = refs[3 + sum(has_far) :]
    tile = lax.axis_index("gy")
    count = own_ref.shape[0] - PAD
    obs = own_ref.shape[1]
    even = lax.rem(tile, 2) == 0
    low_half = lax.rem(tile // 2, 2) == 0
    slots = CP + 2
    far = []
    index = 0
    for there in has_far:
        far.append(far_refs[index][...] if there else None)
        index += 1 if there else 0
    left[:, 2 * obs : 3 * obs] = own_ref[...]
    left[:, obs : 2 * obs] = jnp.where(even, other_ref[...], first_ref[...])
    left[:, 3 * obs : 4 * obs] = jnp.where(even, first_ref[...], other_ref[...])
    blank = jnp.zeros(own_ref.shape, jnp.bfloat16)
    near, beyond = [blank if block is None else block for block in far]
    left[:, 0:obs] = jnp.where(low_half, beyond, near)
    left[:, 4 * obs :] = jnp.where(low_half, near, beyond)
    present = []
    for offset in range(-2, 3):
        present.append(select_flag((tile + offset >= 0) & (tile + offset < size)))
    parts = []
    for slot in range(slots):
        point = slot - 1
        owner = point // CP
        centre = (point + 0.5) * spacing
        bases = [float((owner + step) * rows) for step in (-1, 0, 1)]
        parts.append(
            point_weights(
                left.at[:, (owner + 1) * obs : (owner + 4) * obs],
                count,
                float(rows),
                centre,
                bases,
                present[owner + 1 : owner + 4],
            )
        )
    height = float(rows * size)
    start = (tile * rows).astype(jnp.float32)
    for row in range(rows):
        low = int((row + 0.5) / spacing + 0.5)
        shares = []
        for slot in (low, low + 1):
            place = jnp.clip(start + (row + 0.5), 0.5 * spacing, height - 0.5 * spacing)
            centre = start + (slot - 0.5) * spacing
            shares.append(jnp.maximum(0.0, 1.0 - jnp.abs(place - centre) / spacing))
        mixed = shares[0] * parts[low][0] + shares[1] * parts[low + 1][0]
        mix_ref[row, 0:count, :] = mixed.astype(jnp.bfloat16)
        mean_row = shares[0] * parts[low][2] + shares[1] * parts[low + 1][2]
        high = mean_row.astype(jnp.bfloat16).astype(jnp.float32)
        which = lax.broadcasted_iota(jnp.int32, (PAD, count), 0)
        two = jnp.where(which == 0, high, jnp.where(which == 1, mean_row - high, 0.0))
        mix_ref[row, count:, :] = two.astype(jnp.bfloat16)
        diag = shares[0] * parts[low][1] + shares[1] * parts[low + 1][1]
        diag_ref[row] = jnp.broadcast_to(diag, (8, 128))


def weights(own, first, other, far, size, rows):
    count = own.shape[0] - PAD
    has_far = tuple(block is not None for block in far)
    blocks = [own, first, other] + [block for block in far if block is not None]
    cube = count * count * count
    return pl.pallas_call(
        functools.partial(weights_kernel, size, rows, rows // CP, has_far),
        out_shape=(
            jax.ShapeDtypeStruct((rows, count + PAD, count), jnp.bfloat16),
            jax.ShapeDtypeStruct((rows, 8, 128), jnp.float32),
        ),
        in_specs=[VMEM] * len(blocks),
        out_specs=(VMEM, VMEM),
        scratch_shapes=[pltpu.VMEM((own.shape[0], 5 * own.shape[1]), jnp.bfloat16)],
        compiler_params=pltpu.CompilerParams(vmem_limit_bytes=48 * MIB),
        cost_estimate=pl.CostEstimate(
            flops=24 * cube, bytes_accessed=8 * count * count, transcendentals=0
        ),
        name="weights",
    )(*blocks)


def analyse_kernel(rows, sorted_ref, mix_ref, diag_ref, out_ref, wide):
    parts, _, members, width = sorted_ref.shape
    count = parts * members
    for row in range(rows):
        prior = sorted_ref[:, row].reshape(count, width).astype(jnp.float32)
        mean = jnp.sum(prior, axis=0, keepdims=True) / count
        deviation = (prior - mean).astype(jnp.bfloat16)
        term = jnp.dot(mix_ref[row], deviation, preferred_element_type=jnp.float32)
        shift = mean + term[count : count + 1] + term[count + 1 : count + 2]
        diag = jnp.broadcast_to(diag_ref[row, 0:1, 0:1], (1, width))
        wide[pl.ds(row, count, stride=rows), :] = (
            term[0:count] + diag * deviation.astype(jnp.float32) + shift
        )
    out_ref[...] = wide[...].astype(jnp.bfloat16)


def analyse(blocks, mix, diag):
    parts, rows, members, width = blocks.shape
    count = parts * members
    flat = pl.pallas_call(
        functools.partial(analyse_kernel, rows),
        out_shape=jax.ShapeDtypeStruct((count * rows, width), jnp.bfloat16),
        in_specs=[VMEM] * 3,
        out_specs=VMEM,
        scratch_shapes=[pltpu.VMEM((count * rows, width), jnp.float32)],
        compiler_params=pltpu.CompilerParams(vmem_limit_bytes=24 * MIB),
        name="analyse",
    )(blocks, mix, diag)
    return flat.reshape(count, rows, width)


def on_device(prior_fields, measured_spread, scaled_misfit, sensor_line_inside):
    parts = lax.axis_size("gx")
    size = lax.axis_size("gy")
    count = measured_spread.shape[0]
    rows = prior_fields.shape[1]
    packed, to_send = prepare(
        prior_fields,
        measured_spread.reshape(count, -1),
        scaled_misfit.reshape(1, -1),
        sensor_line_inside.reshape(1, -1),
        parts,
    )

    def trade(pairs):
        return lax.ppermute(packed, "gy", pairs) if pairs else None

    first = trade(swap_pairs(size, 1, 0))
    other = trade(swap_pairs(size, 1, 1))
    far = [trade(swap_pairs(size, 2, 0)), trade(swap_pairs(size, 2, 1))]
    blocks = lax.all_to_all(to_send, "gx", split_axis=0, concat_axis=0, tiled=True)
    mix, diag = weights(packed, first, other, far, size, rows)
    return analyse(blocks, mix, diag)


def solution(mesh):
    return jax.shard_map(
        on_device,
        mesh=mesh,
        in_specs=(P("gx", "gy", None), P(None, "gy", "gx"), P("gy", "gx"), P("gy", "gx")),
        out_specs=P(None, "gy", "gx"),
        check_vma=False,
    )
```

```python
import functools

import jax
import jax.numpy as jnp
from jax import lax
from jax.experimental import pallas as pl
from jax.experimental.pallas import tpu as pltpu
from jax.sharding import PartitionSpec as P

CP = 2
PAD = 16
MIB = 1 << 20

VMEM = pl.BlockSpec(memory_space=pltpu.VMEM)
HBM = pl.BlockSpec(memory_space=pltpu.HBM)


def swap_pairs(size, reach, phase):
    lows = [i for i in range(size - reach) if (i // reach) % 2 == phase]
    return [pair for i in lows for pair in ((i, i + reach), (i + reach, i))]


def pack_kernel(spread_ref, misfit_ref, line_ref, packed_ref, misfit, line, sems):
    count, width = spread_ref.shape
    copies = [
        pltpu.make_async_copy(spread_ref, packed_ref.at[0:count], sems.at[0]),
        pltpu.make_async_copy(misfit_ref, misfit, sems.at[1]),
        pltpu.make_async_copy(line_ref, line, sems.at[2]),
    ]
    for copy in copies:
        copy.start()
    for copy in copies[1:]:
        copy.wait()
    which = lax.broadcasted_iota(jnp.int32, (PAD, width), 0)
    misfits = jnp.broadcast_to(misfit[...].astype(jnp.float32), (PAD, width))
    lines = jnp.broadcast_to(line[...].astype(jnp.float32), (PAD, width))
    extra = jnp.where(which == 0, misfits, jnp.where(which == 1, lines, 0.0))
    packed_ref[count:, :] = extra.astype(jnp.bfloat16)
    copies[0].wait()


def pack(spread, misfit, line):
    count, obs = spread.shape
    return pl.pallas_call(
        pack_kernel,
        out_shape=pltpu.VMEM((count + PAD, obs), jnp.bfloat16),
        in_specs=[HBM] * 3,
        out_specs=VMEM,
        scratch_shapes=[
            pltpu.VMEM(misfit.shape, misfit.dtype),
            pltpu.VMEM(line.shape, line.dtype),
            pltpu.SemaphoreType.DMA((3,)),
        ],
        name="pack",
    )(*[pltpu.with_memory_space_constraint(array, pltpu.HBM) for array in (spread, misfit, line)])


def sort_kernel(parts, rows, prior_ref, sorted_ref, held, wide, sems):
    stride = parts * rows
    members = prior_ref.shape[0] // stride
    step = min(members, PAD)
    chunks = members // step
    copies = []
    for chunk in range(chunks):
        span = pl.ds(chunk * step * stride, step * stride)
        copies.append(pltpu.make_async_copy(prior_ref.at[span], held.at[span], sems.at[chunk]))
        copies[-1].start()
    for chunk in range(chunks):
        span = pl.ds(chunk * step * stride, step * stride)
        copies[chunk].wait()
        wide[span, :] = held[span, :].astype(jnp.float32)
        for part in range(parts):
            for row in range(rows):
                first = chunk * step * stride + part * rows + row
                lines = wide[pl.ds(first, step, stride=stride), :]
                sorted_ref[part, row, pl.ds(chunk * step, step), :] = lines.astype(jnp.bfloat16)


def sort(prior, parts):
    members, rows, cells = prior.shape
    width = cells // parts
    flat = prior.reshape(members, rows, parts, width).transpose(0, 2, 1, 3).reshape(-1, width)
    return pl.pallas_call(
        functools.partial(sort_kernel, parts, rows),
        out_shape=jax.ShapeDtypeStruct((parts, rows, members, width), jnp.bfloat16),
        in_specs=[HBM],
        out_specs=VMEM,
        scratch_shapes=[
            pltpu.VMEM(flat.shape, jnp.bfloat16),
            pltpu.VMEM(flat.shape, jnp.float32),
            pltpu.SemaphoreType.DMA((members // min(members, PAD),)),
        ],
        compiler_params=pltpu.CompilerParams(vmem_limit_bytes=24 * MIB),
        cost_estimate=pl.CostEstimate(flops=0, bytes_accessed=4 * MIB, transcendentals=0),
        name="sort",
    )(pltpu.with_memory_space_constraint(flat, pltpu.HBM))


def select_flag(condition):
    return jnp.where(condition, jnp.float32(1.0), jnp.float32(0.0))


def point_weights(left, count, radius, centre, bases, present):
    line = left[count + 1 : count + 2, :].astype(jnp.float32)
    obs = line.shape[1] // 3
    where = lax.broadcasted_iota(jnp.int32, line.shape, 1) // obs
    base = jnp.where(where == 0, bases[0], jnp.where(where == 1, bases[1], bases[2]))
    alive = jnp.where(where == 0, present[0], jnp.where(where == 1, present[1], present[2]))
    distance = (base + line + 0.5 - centre) / radius
    locality = jnp.exp(-0.5 * distance * distance) * alive
    scaled = (left[0:count, :].astype(jnp.float32) * locality).astype(jnp.bfloat16)
    both = lax.dot_general(
        left[...], scaled, (((1,), (1,)), ((), ())), preferred_element_type=jnp.float32
    )
    gram = both[0:count]
    drive = both[count : count + 1]
    share = 1.0 / (count - 1.0)
    on_diagonal = lax.broadcasted_iota(jnp.int32, gram.shape, 0) == lax.broadcasted_iota(
        jnp.int32, gram.shape, 1
    )
    sizes = jnp.abs(jnp.where(on_diagonal, 1.0, 0.0) + gram * share)
    bound = jnp.max(jnp.sum(sizes, axis=0, keepdims=True), axis=1, keepdims=True)
    rounded = gram.astype(jnp.bfloat16)
    square = jnp.dot(rounded, rounded, preferred_element_type=jnp.float32)
    s = 1.0 / bound
    g = s * share
    first = jnp.broadcast_to(g, (1, count))
    second = jnp.broadcast_to(g * g, (1, count))
    beta = s * s - 9.0 * s
    quad = second * square
    x = (2.0 * s) * first * gram + quad
    w = (2.0 * s - 9.0) * first * gram + quad
    product = jnp.dot(x.astype(jnp.bfloat16), w.astype(jnp.bfloat16), preferred_element_type=jnp.float32)
    on_gram = (-39.0 + (27.0 + beta) * (2.0 * s) + s * s * (2.0 * s - 9.0)) * first / 16.0
    on_square = (27.0 + beta + s * s) * second / 16.0
    rest = on_gram * gram + on_square * square + product * (1.0 / 16.0)
    scalar_part = (36.0 + s * (-39.0 + s * (27.0 + s * (-9.0 + s)))) / 16.0
    rest_rounded = rest.astype(jnp.bfloat16)

    def row_times(row):
        high = row.astype(jnp.bfloat16).astype(jnp.float32)
        which = lax.broadcasted_iota(jnp.int32, (PAD, count), 0)
        two = jnp.where(which == 0, high, jnp.where(which == 1, row - high, 0.0))
        out = jnp.dot(two.astype(jnp.bfloat16), rest_rounded, preferred_element_type=jnp.float32)
        return out[0:1] + out[1:2] + scalar_part * row

    mean_weights = row_times(row_times(drive)) * g
    root = lax.rsqrt(bound)
    return rest * jnp.broadcast_to(root, (1, count)), scalar_part * root, mean_weights


def weights_kernel(size, rows, spacing, has_far, *refs):
    own_ref, first_ref, other_ref = refs[:3]
    far_refs = refs[3 : 3 + sum(has_far)]
    mix_ref, diag_ref, left = refs[3 + sum(has_far) :]
    tile = lax.axis_index("gy")
    count = own_ref.shape[0] - PAD
    obs = own_ref.shape[1]
    even = lax.rem(tile, 2) == 0
    low_half = lax.rem(tile // 2, 2) == 0
    slots = CP + 2
    far = []
    index = 0
    for there in has_far:
        far.append(far_refs[index][...] if there else None)
        index += 1 if there else 0
    left[:, 2 * obs : 3 * obs] = own_ref[...]
    left[:, obs : 2 * obs] = jnp.where(even, other_ref[...], first_ref[...])
    left[:, 3 * obs : 4 * obs] = jnp.where(even, first_ref[...], other_ref[...])
    blank = jnp.zeros(own_ref.shape, jnp.bfloat16)
    near, beyond = [blank if block is None else block for block in far]
    left[:, 0:obs] = jnp.where(low_half, beyond, near)
    left[:, 4 * obs :] = jnp.where(low_half, near, beyond)
    present = []
    for offset in range(-2, 3):
        present.append(select_flag((tile + offset >= 0) & (tile + offset < size)))
    parts = []
    for slot in range(slots):
        point = slot - 1
        owner = point // CP
        centre = (point + 0.5) * spacing
        bases = [float((owner + step) * rows) for step in (-1, 0, 1)]
        parts.append(
            point_weights(
                left.at[:, (owner + 1) * obs : (owner + 4) * obs],
                count,
                float(rows),
                centre,
                bases,
                present[owner + 1 : owner + 4],
            )
        )
    height = float(rows * size)
    start = (tile * rows).astype(jnp.float32)
    for row in range(rows):
        low = int((row + 0.5) / spacing + 0.5)
        shares = []
        for slot in (low, low + 1):
            place = jnp.clip(start + (row + 0.5), 0.5 * spacing, height - 0.5 * spacing)
            centre = start + (slot - 0.5) * spacing
            shares.append(jnp.maximum(0.0, 1.0 - jnp.abs(place - centre) / spacing))
        mixed = shares[0] * parts[low][0] + shares[1] * parts[low + 1][0]
        mix_ref[row, 0:count, :] = mixed.astype(jnp.bfloat16)
        mean_row = shares[0] * parts[low][2] + shares[1] * parts[low + 1][2]
        high = mean_row.astype(jnp.bfloat16).astype(jnp.float32)
        which = lax.broadcasted_iota(jnp.int32, (PAD, count), 0)
        two = jnp.where(which == 0, high, jnp.where(which == 1, mean_row - high, 0.0))
        mix_ref[row, count:, :] = two.astype(jnp.bfloat16)
        diag = shares[0] * parts[low][1] + shares[1] * parts[low + 1][1]
        diag_ref[row] = jnp.broadcast_to(diag, (8, 128))


def weights(own, first, other, far, size, rows):
    count = own.shape[0] - PAD
    has_far = tuple(block is not None for block in far)
    blocks = [own, first, other] + [block for block in far if block is not None]
    cube = count * count * count
    return pl.pallas_call(
        functools.partial(weights_kernel, size, rows, rows // CP, has_far),
        out_shape=(
            jax.ShapeDtypeStruct((rows, count + PAD, count), jnp.bfloat16),
            jax.ShapeDtypeStruct((rows, 8, 128), jnp.float32),
        ),
        in_specs=[VMEM] * len(blocks),
        out_specs=(VMEM, VMEM),
        scratch_shapes=[pltpu.VMEM((own.shape[0], 5 * own.shape[1]), jnp.bfloat16)],
        compiler_params=pltpu.CompilerParams(vmem_limit_bytes=48 * MIB),
        cost_estimate=pl.CostEstimate(
            flops=240 * cube, bytes_accessed=8 * count * count, transcendentals=0
        ),
        name="weights",
    )(*blocks)


def analyse_kernel(rows, sorted_ref, mix_ref, diag_ref, out_ref, wide):
    parts, _, members, width = sorted_ref.shape
    count = parts * members
    for row in range(rows):
        prior = sorted_ref[:, row].reshape(count, width).astype(jnp.float32)
        mean = jnp.sum(prior, axis=0, keepdims=True) / count
        deviation = (prior - mean).astype(jnp.bfloat16)
        term = jnp.dot(mix_ref[row], deviation, preferred_element_type=jnp.float32)
        shift = mean + term[count : count + 1] + term[count + 1 : count + 2]
        diag = jnp.broadcast_to(diag_ref[row, 0:1, 0:1], (1, width))
        wide[pl.ds(row, count, stride=rows), :] = (
            term[0:count] + diag * deviation.astype(jnp.float32) + shift
        )
    out_ref[...] = wide[...].astype(jnp.bfloat16)


def analyse(blocks, mix, diag):
    parts, rows, members, width = blocks.shape
    count = parts * members
    flat = pl.pallas_call(
        functools.partial(analyse_kernel, rows),
        out_shape=jax.ShapeDtypeStruct((count * rows, width), jnp.bfloat16),
        in_specs=[VMEM] * 3,
        out_specs=VMEM,
        scratch_shapes=[pltpu.VMEM((count * rows, width), jnp.float32)],
        compiler_params=pltpu.CompilerParams(vmem_limit_bytes=24 * MIB),
        name="analyse",
    )(blocks, mix, diag)
    return flat.reshape(count, rows, width)


def on_device(prior_fields, measured_spread, scaled_misfit, sensor_line_inside):
    parts = lax.axis_size("gx")
    size = lax.axis_size("gy")
    count = measured_spread.shape[0]
    rows = prior_fields.shape[1]
    packed = pack(
        measured_spread.reshape(count, -1),
        scaled_misfit.reshape(1, -1),
        sensor_line_inside.reshape(1, -1),
    )
    to_send = sort(prior_fields, parts)

    def trade(pairs):
        return lax.ppermute(packed, "gy", pairs) if pairs else None

    first = trade(swap_pairs(size, 1, 0))
    other = trade(swap_pairs(size, 1, 1))
    far = [trade(swap_pairs(size, 2, 0)), trade(swap_pairs(size, 2, 1))]
    blocks = lax.all_to_all(to_send, "gx", split_axis=0, concat_axis=0, tiled=True)
    mix, diag = weights(packed, first, other, far, size, rows)
    return analyse(blocks, mix, diag)


def solution(mesh):
    return jax.shard_map(
        on_device,
        mesh=mesh,
        in_specs=(P("gx", "gy", None), P(None, "gy", "gx"), P("gy", "gx"), P("gy", "gx")),
        out_specs=P(None, "gy", "gx"),
        check_vma=False,
    )
```

```python
import functools

import jax
import jax.numpy as jnp
from jax import lax
from jax.experimental import pallas as pl
from jax.experimental.pallas import tpu as pltpu
from jax.sharding import PartitionSpec as P

CP = 2
PAD = 16
MIB = 1 << 20
NEAR_FLOPS = 180
FAR_FLOPS = 2

VMEM = pl.BlockSpec(memory_space=pltpu.VMEM)
HBM = pl.BlockSpec(memory_space=pltpu.HBM)


def swap_pairs(size, reach, phase):
    lows = [i for i in range(size - reach) if (i // reach) % 2 == phase]
    return [pair for i in lows for pair in ((i, i + reach), (i + reach, i))]


def target_chip(chip, step, chips):
    if chips & (chips - 1) == 0:
        return chip ^ step
    return (chip + step) % chips if isinstance(chip, int) else lax.rem(chip + step, chips)


def source_chip(chip, step, chips):
    return target_chip(chip, step if chips & (chips - 1) == 0 else chips - step, chips)


def split_kernel(chips, prior_ref, spread_ref, misfit_ref, line_ref, *refs):
    packed_ref, keep_ref, give_ref, misfit, line, sems = refs
    count, width = spread_ref.shape
    copies = [
        pltpu.make_async_copy(spread_ref, packed_ref.at[0:count], sems.at[0]),
        pltpu.make_async_copy(misfit_ref, misfit, sems.at[1]),
        pltpu.make_async_copy(line_ref, line, sems.at[2]),
    ]
    core = lax.rem(lax.axis_index("gx"), 2)
    cells = prior_ref.shape[2] // (2 * chips)
    for chip in range(chips):
        for place, (side, ref) in enumerate(((core, keep_ref), (1 - core, give_ref))):
            first = pl.multiple_of((2 * chip + side) * cells, cells)
            copies.append(
                pltpu.make_async_copy(
                    prior_ref.at[:, :, pl.ds(first, cells)],
                    ref.at[chip],
                    sems.at[3 + 2 * chip + place],
                )
            )
    for copy in copies:
        copy.start()
    for copy in copies[1:3]:
        copy.wait()
    which = lax.broadcasted_iota(jnp.int32, (PAD, width), 0)
    misfits = jnp.broadcast_to(misfit[...].astype(jnp.float32), (PAD, width))
    lines = jnp.broadcast_to(line[...].astype(jnp.float32), (PAD, width))
    extra = jnp.where(which == 0, misfits, jnp.where(which == 1, lines, 0.0))
    packed_ref[count:, :] = extra.astype(jnp.bfloat16)
    copies[0].wait()
    for copy in copies[3:]:
        copy.wait()


def split(prior, spread, misfit, line, chips):
    members, rows, cells = prior.shape
    count, obs = spread.shape
    half = (chips, members, rows, cells // (2 * chips))
    inputs = (prior, spread, misfit, line)
    return pl.pallas_call(
        functools.partial(split_kernel, chips),
        out_shape=(
            pltpu.VMEM((count + PAD, obs), jnp.bfloat16),
            pltpu.VMEM(half, jnp.bfloat16),
            pltpu.VMEM(half, jnp.bfloat16),
        ),
        in_specs=[HBM] * 4,
        out_specs=(VMEM,) * 3,
        scratch_shapes=[
            pltpu.VMEM(misfit.shape, misfit.dtype),
            pltpu.VMEM(line.shape, line.dtype),
            pltpu.SemaphoreType.DMA((3 + 2 * chips,)),
        ],
        name="split",
    )(*[pltpu.with_memory_space_constraint(array, pltpu.HBM) for array in inputs])


def sort_kernel(chips, rows, keep_ref, got_ref, *refs):
    sorted_refs, wide = refs[:chips], refs[chips]
    members = keep_ref.shape[0] // (chips * rows)
    index = lax.axis_index("gx")
    core = lax.rem(index, 2)
    chip = index // 2
    for half, ref in enumerate((keep_ref, got_ref)):
        wide[half] = ref[...].astype(jnp.float32)
    for step in range(chips):
        first = target_chip(chip, step, chips) * (members * rows)
        for half, side in enumerate((core, 1 - core)):
            for row in range(rows):
                lines = wide[half, pl.ds(first + row, members, stride=rows), :]
                sorted_refs[step][side, row] = lines.astype(jnp.bfloat16)


def sort(keep, got):
    chips, members, rows, cells = keep.shape
    flat = (chips * members * rows, cells)
    return pl.pallas_call(
        functools.partial(sort_kernel, chips, rows),
        out_shape=[pltpu.VMEM((2, rows, members, cells), jnp.bfloat16)] * chips,
        in_specs=[VMEM] * 2,
        out_specs=[VMEM] * chips,
        scratch_shapes=[pltpu.VMEM((2,) + flat, jnp.float32)],
        compiler_params=pltpu.CompilerParams(vmem_limit_bytes=16 * MIB),
        cost_estimate=pl.CostEstimate(flops=0, bytes_accessed=4 * MIB, transcendentals=0),
        name="sort",
    )(keep.reshape(flat), got.reshape(flat))


def select_flag(condition):
    return jnp.where(condition, jnp.float32(1.0), jnp.float32(0.0))


def point_weights(left, count, radius, centre, bases, present):
    line = left[count + 1 : count + 2, :].astype(jnp.float32)
    obs = line.shape[1] // 3
    where = lax.broadcasted_iota(jnp.int32, line.shape, 1) // obs
    base = jnp.where(where == 0, bases[0], jnp.where(where == 1, bases[1], bases[2]))
    alive = jnp.where(where == 0, present[0], jnp.where(where == 1, present[1], present[2]))
    distance = (base + line + 0.5 - centre) / radius
    locality = jnp.exp(-0.5 * distance * distance) * alive
    scaled = (left[0:count, :].astype(jnp.float32) * locality).astype(jnp.bfloat16)
    both = lax.dot_general(
        left[...], scaled, (((1,), (1,)), ((), ())), preferred_element_type=jnp.float32
    )
    gram = both[0:count]
    drive = both[count : count + 1]
    share = 1.0 / (count - 1.0)
    on_diagonal = lax.broadcasted_iota(jnp.int32, gram.shape, 0) == lax.broadcasted_iota(
        jnp.int32, gram.shape, 1
    )
    sizes = jnp.abs(jnp.where(on_diagonal, 1.0, 0.0) + gram * share)
    bound = jnp.max(jnp.sum(sizes, axis=0, keepdims=True), axis=1, keepdims=True)
    rounded = gram.astype(jnp.bfloat16)
    square = jnp.dot(rounded, rounded, preferred_element_type=jnp.float32)
    s = 1.0 / bound
    g = s * share
    first = jnp.broadcast_to(g, (1, count))
    second = jnp.broadcast_to(g * g, (1, count))
    beta = s * s - 9.0 * s
    quad = second * square
    x = (2.0 * s) * first * gram + quad
    w = (2.0 * s - 9.0) * first * gram + quad
    product = jnp.dot(x.astype(jnp.bfloat16), w.astype(jnp.bfloat16), preferred_element_type=jnp.float32)
    on_gram = (-39.0 + (27.0 + beta) * (2.0 * s) + s * s * (2.0 * s - 9.0)) * first / 16.0
    on_square = (27.0 + beta + s * s) * second / 16.0
    rest = on_gram * gram + on_square * square + product * (1.0 / 16.0)
    scalar_part = (36.0 + s * (-39.0 + s * (27.0 + s * (-9.0 + s)))) / 16.0
    rest_rounded = rest.astype(jnp.bfloat16)

    def row_times(row):
        out = jnp.dot(two_rows(row), rest_rounded, preferred_element_type=jnp.float32)
        return out[0:1] + out[1:2] + scalar_part * row

    mean_weights = row_times(row_times(drive)) * g
    root = lax.rsqrt(bound)
    return rest * jnp.broadcast_to(root, (1, count)), scalar_part * root, mean_weights


def two_rows(row):
    high = row.astype(jnp.bfloat16).astype(jnp.float32)
    which = lax.broadcasted_iota(jnp.int32, (PAD, row.shape[1]), 0)
    return jnp.where(which == 0, high, jnp.where(which == 1, row - high, 0.0)).astype(jnp.bfloat16)


class Place:
    def __init__(self, size, rows):
        self.size, self.rows = size, rows
        self.spacing = rows // CP
        self.edge = self.spacing // 2
        self.tile = lax.axis_index("gy")
        self.upward = lax.rem(self.tile // 2, 2) == 0
        self.even = lax.rem(self.tile, 2) == 0
        self.sign = jnp.where(self.upward, 1, -1)

    def present(self, offset):
        there = (self.tile + offset >= 0) & (self.tile + offset < self.size)
        return select_flag(there)

    def share(self, row, point):
        start = (self.tile * self.rows).astype(jnp.float32)
        height = float(self.rows * self.size)
        place = jnp.clip(start + row + 0.5, 0.5 * self.spacing, height - 0.5 * self.spacing)
        centre = start + (point + 0.5) * self.spacing
        return jnp.maximum(0.0, 1.0 - jnp.abs(place - centre) / self.spacing)

    def edge_row(self, ahead, step):
        first, last = step, self.rows - 1 - step
        return jnp.where(self.upward == ahead, last, first)

    def side_point(self, ahead):
        return jnp.where(self.upward == ahead, jnp.float32(CP), jnp.float32(-1))

    def own_point(self, ahead):
        return jnp.where(self.upward == ahead, jnp.float32(CP - 1), jnp.float32(0))

    def side(self, left, count, ahead):
        sign = self.sign if ahead else -self.sign
        offsets = (sign, 2 * sign, 0 * sign)
        bases = [(offset * self.rows).astype(jnp.float32) for offset in offsets]
        present = [self.present(offset) for offset in offsets]
        centre = (self.side_point(ahead) + 0.5) * self.spacing
        return point_weights(left, count, float(self.rows), centre, bases, present)


def write_mix(mix_ref, diag_ref, row, terms, count):
    mix_ref[row, 0:count, :] = sum(share * part[0] for share, part in terms).astype(jnp.bfloat16)
    mix_ref[row, count:, :] = two_rows(sum(share * part[2] for share, part in terms))
    diag_ref[row] = jnp.broadcast_to(sum(share * part[1] for share, part in terms), (8, 128))


def near_kernel(size, rows, has_far, *refs):
    own_ref, first_ref, other_ref = refs[:3]
    mix_ref, diag_ref, beside_ref, small_ref, left = refs[4 if has_far else 3 :]
    count, obs = own_ref.shape[0] - PAD, own_ref.shape[1]
    at = Place(size, rows)
    ahead_is_first = at.even == at.upward
    left[:, 0:obs] = jnp.where(ahead_is_first, first_ref[...], other_ref[...])
    left[:, obs : 2 * obs] = own_ref[...]
    left[:, 2 * obs : 3 * obs] = jnp.where(ahead_is_first, other_ref[...], first_ref[...])
    far = refs[3][...] if has_far else jnp.zeros(own_ref.shape, jnp.bfloat16)
    left[:, 3 * obs : 4 * obs] = far
    left[:, 4 * obs :] = own_ref[...]
    offsets = (at.sign, 0 * at.sign, -at.sign)
    bases = [(offset * rows).astype(jnp.float32) for offset in offsets]
    present = [at.present(offset) for offset in offsets]
    own = []
    for point in range(CP):
        centre = (point + 0.5) * at.spacing
        own.append(
            point_weights(left.at[:, 0 : 3 * obs], count, float(rows), centre, bases, present)
        )
    behind = at.side(left.at[:, 2 * obs :], count, False)
    for row in range(at.edge, rows - at.edge):
        low = int((row + 0.5) / at.spacing - 0.5)
        terms = [(at.share(row, low + step), own[low + step]) for step in (0, 1)]
        write_mix(mix_ref, diag_ref, row, terms, count)

    def pick(ahead):
        flag = at.upward == ahead
        return [jnp.where(flag, last, first) for first, last in zip(own[0], own[CP - 1])]

    for step in range(at.edge):
        row = at.edge_row(False, step)
        terms = [
            (at.share(row, at.own_point(False)), pick(False)),
            (at.share(row, at.side_point(False)), behind),
        ]
        write_mix(mix_ref, diag_ref, row, terms, count)
    beside = pick(True)
    beside_ref[...] = beside[0]
    small_ref[0:8, :] = jnp.broadcast_to(beside[1], (8, count))
    small_ref[8:16, :] = jnp.broadcast_to(beside[2], (8, count))


def far_kernel(size, rows, own_ref, first_ref, other_ref, far_ref, beside_ref, small_ref, *refs):
    mix_ref, diag_ref, left = refs
    count, obs = own_ref.shape[0] - PAD, own_ref.shape[1]
    at = Place(size, rows)
    left[:, 0:obs] = jnp.where(at.even == at.upward, first_ref[...], other_ref[...])
    left[:, obs : 2 * obs] = far_ref[...]
    left[:, 2 * obs :] = own_ref[...]
    ahead = at.side(left, count, True)
    beside = (beside_ref[...], small_ref[0:1, 0:1], small_ref[8:9, :])
    for step in range(at.edge):
        row = at.edge_row(True, step)
        terms = [
            (at.share(row, at.own_point(True)), beside),
            (at.share(row, at.side_point(True)), ahead),
        ]
        write_mix(mix_ref, diag_ref, step, terms, count)


def weights(own, first, other, far, beyond, size, rows):
    count, obs = own.shape[0] - PAD, own.shape[1]
    edge = rows // CP // 2
    near_inputs = [own, first, other] + ([] if beyond is None else [beyond])
    mix, diag, beside, small = pl.pallas_call(
        functools.partial(near_kernel, size, rows, beyond is not None),
        out_shape=(
            pltpu.VMEM((rows, count + PAD, count), jnp.bfloat16),
            pltpu.VMEM((rows, 8, 128), jnp.float32),
            pltpu.VMEM((count, count), jnp.float32),
            pltpu.VMEM((16, count), jnp.float32),
        ),
        in_specs=[VMEM] * len(near_inputs),
        out_specs=(VMEM,) * 4,
        scratch_shapes=[pltpu.VMEM((count + PAD, 5 * obs), jnp.bfloat16)],
        compiler_params=pltpu.CompilerParams(vmem_limit_bytes=40 * MIB),
        cost_estimate=pl.CostEstimate(
            flops=NEAR_FLOPS * count**3, bytes_accessed=8 * count * count, transcendentals=0
        ),
        name="near",
    )(*near_inputs)
    edge_mix, edge_diag = pl.pallas_call(
        functools.partial(far_kernel, size, rows),
        out_shape=(
            pltpu.VMEM((edge, count + PAD, count), jnp.bfloat16),
            pltpu.VMEM((edge, 8, 128), jnp.float32),
        ),
        in_specs=[VMEM] * 6,
        out_specs=(VMEM,) * 2,
        scratch_shapes=[pltpu.VMEM((count + PAD, 3 * obs), jnp.bfloat16)],
        compiler_params=pltpu.CompilerParams(vmem_limit_bytes=32 * MIB),
        cost_estimate=pl.CostEstimate(
            flops=FAR_FLOPS * count**3, bytes_accessed=8 * count * count, transcendentals=0
        ),
        name="far",
    )(own, first, other, far, beside, small)
    return mix, diag, edge_mix, edge_diag


def analyse_kernel(size, *refs):
    mix_ref, diag_ref, edge_mix_ref, edge_diag_ref = refs[:4]
    block_refs = refs[4:-3]
    out_ref, deviations, wide = refs[-3:]
    chips = len(block_refs)
    _, rows, members, width = block_refs[0].shape
    count = 2 * chips * members
    at = Place(size, rows)
    chip = lax.axis_index("gx") // 2

    def one_row(row, mix, diag):
        halves = [(step, side) for step in range(chips) for side in range(2)]
        blocks = [block_refs[step][side, row].astype(jnp.float32) for step, side in halves]
        total = sum(jnp.sum(block, axis=0, keepdims=True) for block in blocks)
        mean = total / count
        for (step, side), block in zip(halves, blocks):
            first = (2 * source_chip(chip, step, chips) + side) * members
            deviations[pl.ds(pl.multiple_of(first, members), members), :] = (block - mean).astype(
                jnp.bfloat16
            )
        deviation = deviations[...]
        term = jnp.dot(mix, deviation, preferred_element_type=jnp.float32)
        shift = mean + term[count : count + 1] + term[count + 1 : count + 2]
        wide[pl.ds(row, count, stride=rows), :] = (
            term[0:count] + diag * deviation.astype(jnp.float32) + shift
        )

    for row in range(at.edge, rows - at.edge):
        one_row(row, mix_ref[row], diag_ref[row, 0:1, 0:width])
    for step in range(at.edge):
        row = at.edge_row(False, step)
        one_row(row, mix_ref[row], diag_ref[row, 0:1, 0:width])
    for step in range(at.edge):
        row = at.edge_row(True, step)
        one_row(row, edge_mix_ref[step], edge_diag_ref[step, 0:1, 0:width])
    out_ref[...] = wide[...].astype(jnp.bfloat16)


def analyse(blocks, mixes, size):
    _, rows, members, width = blocks[0].shape
    count = 2 * len(blocks) * members
    flat = pl.pallas_call(
        functools.partial(analyse_kernel, size),
        out_shape=jax.ShapeDtypeStruct((count * rows, width), jnp.bfloat16),
        in_specs=[VMEM] * (4 + len(blocks)),
        out_specs=VMEM,
        scratch_shapes=[
            pltpu.VMEM((count, width), jnp.bfloat16),
            pltpu.VMEM((count * rows, width), jnp.float32),
        ],
        compiler_params=pltpu.CompilerParams(vmem_limit_bytes=24 * MIB),
        name="analyse",
    )(*mixes, *blocks)
    return flat.reshape(count, rows, width)


def on_device(prior_fields, measured_spread, scaled_misfit, sensor_line_inside):
    parts = lax.axis_size("gx")
    chips = parts // 2
    size = lax.axis_size("gy")
    count = measured_spread.shape[0]
    rows = prior_fields.shape[1]
    packed, keep, give = split(
        prior_fields,
        measured_spread.reshape(count, -1),
        scaled_misfit.reshape(1, -1),
        sensor_line_inside.reshape(1, -1),
        chips,
    )

    def trade(pairs):
        return lax.ppermute(packed, "gy", pairs) if pairs else None

    got = lax.ppermute(give, "gx", [(index, index ^ 1) for index in range(parts)])
    first = trade(swap_pairs(size, 1, 0))
    other = trade(swap_pairs(size, 1, 1))
    far, beyond = trade(swap_pairs(size, 2, 0)), trade(swap_pairs(size, 2, 1))
    own, *sent = sort(keep, got)
    blocks = [own]
    for step, block in enumerate(sent, 1):
        pairs = [
            (index, 2 * target_chip(index // 2, step, chips) + index % 2) for index in range(parts)
        ]
        blocks.append(lax.ppermute(block, "gx", pairs))
    mixes = weights(packed, first, other, far, beyond, size, rows)
    return analyse(blocks, mixes, size)


def solution(mesh):
    return jax.shard_map(
        on_device,
        mesh=mesh,
        in_specs=(P("gx", "gy", None), P(None, "gy", "gx"), P("gy", "gx"), P("gy", "gx")),
        out_specs=P(None, "gy", "gx"),
        check_vma=False,
    )
```

```python
import functools

import jax
import jax.numpy as jnp
from jax import lax
from jax.experimental import pallas as pl
from jax.experimental.pallas import tpu as pltpu
from jax.sharding import PartitionSpec as P

CP = 2
PAD = 16
MIB = 1 << 20
NEAR_FLOPS = 180
FAR_FLOPS = 2

VMEM = pl.BlockSpec(memory_space=pltpu.VMEM)
HBM = pl.BlockSpec(memory_space=pltpu.HBM)


def swap_pairs(size, reach, phase):
    lows = [i for i in range(size - reach) if (i // reach) % 2 == phase]
    return [pair for i in lows for pair in ((i, i + reach), (i + reach, i))]


def target_chip(chip, step, chips):
    if chips & (chips - 1) == 0:
        return chip ^ step
    return (chip + step) % chips if isinstance(chip, int) else lax.rem(chip + step, chips)


def source_chip(chip, step, chips):
    return target_chip(chip, step if chips & (chips - 1) == 0 else chips - step, chips)


def split_kernel(chips, prior_ref, spread_ref, misfit_ref, line_ref, *refs):
    packed_ref, keep_ref, give_ref, misfit, line, sems = refs
    count, width = spread_ref.shape
    copies = [
        pltpu.make_async_copy(spread_ref, packed_ref.at[0:count], sems.at[0]),
        pltpu.make_async_copy(misfit_ref, misfit, sems.at[1]),
        pltpu.make_async_copy(line_ref, line, sems.at[2]),
    ]
    core = lax.rem(lax.axis_index("gx"), 2)
    cells = prior_ref.shape[2] // (2 * chips)
    for chip in range(chips):
        for place, (side, ref) in enumerate(((core, keep_ref), (1 - core, give_ref))):
            first = pl.multiple_of((2 * chip + side) * cells, cells)
            copies.append(
                pltpu.make_async_copy(
                    prior_ref.at[:, :, pl.ds(first, cells)],
                    ref.at[chip],
                    sems.at[3 + 2 * chip + place],
                )
            )
    for copy in copies:
        copy.start()
    for copy in copies[1:3]:
        copy.wait()
    which = lax.broadcasted_iota(jnp.int32, (PAD, width), 0)
    misfits = jnp.broadcast_to(misfit[...].astype(jnp.float32), (PAD, width))
    lines = jnp.broadcast_to(line[...].astype(jnp.float32), (PAD, width))
    extra = jnp.where(which == 0, misfits, jnp.where(which == 1, lines, 0.0))
    packed_ref[count:, :] = extra.astype(jnp.bfloat16)
    copies[0].wait()
    for copy in copies[3:]:
        copy.wait()


def split(prior, spread, misfit, line, chips):
    members, rows, cells = prior.shape
    count, obs = spread.shape
    half = (chips, members, rows, cells // (2 * chips))
    inputs = (prior, spread, misfit, line)
    return pl.pallas_call(
        functools.partial(split_kernel, chips),
        out_shape=(
            pltpu.VMEM((count + PAD, obs), jnp.bfloat16),
            pltpu.VMEM(half, jnp.bfloat16),
            pltpu.VMEM(half, jnp.bfloat16),
        ),
        in_specs=[HBM] * 4,
        out_specs=(VMEM,) * 3,
        scratch_shapes=[
            pltpu.VMEM(misfit.shape, misfit.dtype),
            pltpu.VMEM(line.shape, line.dtype),
            pltpu.SemaphoreType.DMA((3 + 2 * chips,)),
        ],
        name="split",
    )(*[pltpu.with_memory_space_constraint(array, pltpu.HBM) for array in inputs])


def sort_kernel(chips, rows, keep_ref, got_ref, *refs):
    sorted_refs, wide = refs[:chips], refs[chips]
    members = keep_ref.shape[0] // (chips * rows)
    index = lax.axis_index("gx")
    core = lax.rem(index, 2)
    chip = index // 2
    for half, ref in enumerate((keep_ref, got_ref)):
        wide[half] = ref[...].astype(jnp.float32)
    for step in range(chips):
        first = target_chip(chip, step, chips) * (members * rows)
        for half, side in enumerate((core, 1 - core)):
            for row in range(rows):
                lines = wide[half, pl.ds(first + row, members, stride=rows), :]
                sorted_refs[step][side, row] = lines.astype(jnp.bfloat16)


def sort(keep, got):
    chips, members, rows, cells = keep.shape
    flat = (chips * members * rows, cells)
    return pl.pallas_call(
        functools.partial(sort_kernel, chips, rows),
        out_shape=[pltpu.VMEM((2, rows, members, cells), jnp.bfloat16)] * chips,
        in_specs=[VMEM] * 2,
        out_specs=[VMEM] * chips,
        scratch_shapes=[pltpu.VMEM((2,) + flat, jnp.float32)],
        compiler_params=pltpu.CompilerParams(vmem_limit_bytes=16 * MIB),
        cost_estimate=pl.CostEstimate(flops=0, bytes_accessed=4 * MIB, transcendentals=0),
        name="sort",
    )(keep.reshape(flat), got.reshape(flat))


def select_flag(condition):
    return jnp.where(condition, jnp.float32(1.0), jnp.float32(0.0))


class Point:
    def __init__(self, left, centre, bases, present):
        self.left, self.centre, self.bases, self.present = left, centre, bases, present


def turn(row, eye):
    block = eye.shape[0]
    pieces = [row[:, i : i + block] for i in range(0, row.shape[1], block)]
    return jnp.concatenate(
        [jnp.sum(eye * piece, axis=1, keepdims=True) for piece in pieces], axis=0
    )


def lay(column, eye):
    block = eye.shape[0]
    pieces = [column[i : i + block] for i in range(0, column.shape[0], block)]
    return jnp.concatenate(
        [jnp.sum(eye * piece, axis=0, keepdims=True) for piece in pieces], axis=1
    )


def point_weights(points, count, radius, gram_ref, square_ref, last_ref, rest_ref):
    share = 1.0 / (count - 1.0)
    slots = range(len(points))
    block = min(count, 128)
    eye = jnp.where(
        lax.broadcasted_iota(jnp.int32, (block, block), 0)
        == lax.broadcasted_iota(jnp.int32, (block, block), 1),
        1.0,
        0.0,
    )
    drives, bounds = [], []
    for slot in slots:
        point = points[slot]
        left = point.left
        line = left[count + 1 : count + 2, :].astype(jnp.float32)
        obs = line.shape[1] // 3
        where = lax.broadcasted_iota(jnp.int32, line.shape, 1) // obs
        first, second, third = point.bases
        base = jnp.where(where == 0, first, jnp.where(where == 1, second, third))
        first, second, third = point.present
        alive = jnp.where(where == 0, first, jnp.where(where == 1, second, third))
        distance = (base + line + 0.5 - point.centre) / radius
        locality = jnp.exp(-0.5 * distance * distance) * alive
        scaled = (left[0:count, :].astype(jnp.float32) * locality).astype(jnp.bfloat16)
        both = lax.dot_general(
            left[...], scaled, (((1,), (1,)), ((), ())), preferred_element_type=jnp.float32
        )
        gram = both[0:count]
        drives.append(both[count : count + 1])
        gram_ref[slot] = gram.astype(jnp.bfloat16)
        sizes = jnp.sum(jnp.abs(gram), axis=0, keepdims=True)
        bounds.append(1.0 + share * jnp.max(sizes, axis=1, keepdims=True))
    factors = []
    for slot in slots:
        s = 1.0 / bounds[slot]
        g = s * share
        root = lax.rsqrt(bounds[slot])
        wide = lambda value: jnp.broadcast_to(value, (1, count))
        third = wide((4.0 * s - 9.0) * (g * g) * g * (root / 16.0))
        fourth = wide((g * g) * (g * g) * (root / 16.0))
        linear = wide((-39.0 + s * (54.0 + s * (-27.0 + 4.0 * s))) * g * (root / 16.0))
        quadratic = wide((27.0 + s * (-27.0 + 6.0 * s)) * (g * g) * (root / 16.0))
        scalar_part = (36.0 + s * (-39.0 + s * (27.0 + s * (-9.0 + s)))) * (root / 16.0)
        factors.append((linear, quadratic, scalar_part, g * bounds[slot]))
        gram = gram_ref[slot]
        square = jnp.dot(gram, gram, preferred_element_type=jnp.float32)
        square_ref[slot] = square.astype(jnp.bfloat16)
        last = third * gram.astype(jnp.float32) + fourth * square
        last_ref[slot] = last.astype(jnp.bfloat16)
    firsts = []
    for slot in slots:
        linear, quadratic, scalar_part, _ = factors[slot]
        product = jnp.dot(square_ref[slot], last_ref[slot], preferred_element_type=jnp.float32)
        rest = (
            linear * gram_ref[slot].astype(jnp.float32)
            + quadratic * square_ref[slot].astype(jnp.float32)
            + product
        )
        rest_ref[slot] = rest.astype(jnp.bfloat16)

    results = []
    for slot in slots:
        _, _, scalar_part, g = factors[slot]
        mean_weights = drives[slot]
        for _ in range(2):
            out = jnp.dot(two_rows(mean_weights), rest_ref[slot], preferred_element_type=jnp.float32)
            mean_weights = out[0:1] + out[1:2] + scalar_part * mean_weights
        mean_weights = mean_weights * g
        results.append((scalar_part, mean_weights))
    return results


def two_rows(row):
    high = row.astype(jnp.bfloat16).astype(jnp.float32)
    which = lax.broadcasted_iota(jnp.int32, (PAD, row.shape[1]), 0)
    return jnp.where(which == 0, high, jnp.where(which == 1, row - high, 0.0)).astype(jnp.bfloat16)


class Place:
    def __init__(self, size, rows):
        self.size, self.rows = size, rows
        self.spacing = rows // CP
        self.edge = self.spacing // 2
        self.tile = lax.axis_index("gy")
        self.upward = lax.rem(self.tile // 2, 2) == 0
        self.even = lax.rem(self.tile, 2) == 0
        self.sign = jnp.where(self.upward, 1, -1)

    def present(self, offset):
        there = (self.tile + offset >= 0) & (self.tile + offset < self.size)
        return select_flag(there)

    def share(self, row, point):
        start = (self.tile * self.rows).astype(jnp.float32)
        height = float(self.rows * self.size)
        place = jnp.clip(start + row + 0.5, 0.5 * self.spacing, height - 0.5 * self.spacing)
        centre = start + (point + 0.5) * self.spacing
        return jnp.maximum(0.0, 1.0 - jnp.abs(place - centre) / self.spacing)

    def edge_row(self, ahead, step):
        first, last = step, self.rows - 1 - step
        return jnp.where(self.upward == ahead, last, first)

    def side_point(self, ahead):
        return jnp.where(self.upward == ahead, jnp.float32(CP), jnp.float32(-1))

    def own_point(self, ahead):
        return jnp.where(self.upward == ahead, jnp.float32(CP - 1), jnp.float32(0))

    def side(self, left, ahead):
        sign = self.sign if ahead else -self.sign
        offsets = (sign, 2 * sign, 0 * sign)
        centre = (self.side_point(ahead) + 0.5) * self.spacing
        return self.point(left, centre, offsets)

    def point(self, left, centre, offsets):
        bases = [(offset * self.rows).astype(jnp.float32) for offset in offsets]
        return Point(left, centre, bases, [self.present(offset) for offset in offsets])


def write_mix(mix_ref, diag_ref, row, terms, count):
    mixed = sum(share * rest.astype(jnp.float32) for share, rest, _, _ in terms)
    mix_ref[row, 0:count, :] = mixed.astype(jnp.bfloat16)
    mix_ref[row, count:, :] = two_rows(sum(share * mean for share, _, _, mean in terms))
    diag_ref[row] = jnp.broadcast_to(sum(share * diag for share, _, diag, _ in terms), (8, 128))


def near_kernel(size, rows, has_far, *refs):
    own_ref, first_ref, other_ref = refs[:3]
    mix_ref, diag_ref, beside_ref, small_ref, left, gram, square, last, rest = refs[
        4 if has_far else 3 :
    ]
    count, obs = own_ref.shape[0] - PAD, own_ref.shape[1]
    at = Place(size, rows)
    ahead_is_first = at.even == at.upward
    left[:, 0:obs] = jnp.where(ahead_is_first, first_ref[...], other_ref[...])
    left[:, obs : 2 * obs] = own_ref[...]
    left[:, 2 * obs : 3 * obs] = jnp.where(ahead_is_first, other_ref[...], first_ref[...])
    far = refs[3][...] if has_far else jnp.zeros(own_ref.shape, jnp.bfloat16)
    left[:, 3 * obs : 4 * obs] = far
    left[:, 4 * obs :] = own_ref[...]
    offsets = (at.sign, 0 * at.sign, -at.sign)
    points = []
    for point in range(CP):
        points.append(at.point(left.at[:, 0 : 3 * obs], (point + 0.5) * at.spacing, offsets))
    points.append(at.side(left.at[:, 2 * obs :], False))
    results = point_weights(points, count, float(rows), gram, square, last, rest)

    def term(row, point, slot):
        return (at.share(row, point), rest[slot], *results[slot])

    for row in range(at.edge, rows - at.edge):
        low = int((row + 0.5) / at.spacing - 0.5)
        terms = [term(row, low + step, low + step) for step in (0, 1)]
        write_mix(mix_ref, diag_ref, row, terms, count)
    for step in range(at.edge):
        row = at.edge_row(False, step)
        terms = [term(row, point, point) for point in range(CP)]
        terms.append(term(row, at.side_point(False), CP))
        write_mix(mix_ref, diag_ref, row, terms, count)
    for point in range(CP):
        beside_ref[point] = rest[point]
        scalar_part, mean_weights = results[point]
        small_ref[point, 0:8, :] = jnp.broadcast_to(scalar_part, (8, count))
        small_ref[point, 8:16, :] = jnp.broadcast_to(mean_weights, (8, count))


def far_kernel(size, rows, own_ref, first_ref, other_ref, far_ref, beside_ref, small_ref, *refs):
    mix_ref, diag_ref, left, gram, square, last, rest = refs
    count, obs = own_ref.shape[0] - PAD, own_ref.shape[1]
    at = Place(size, rows)
    left[:, 0:obs] = jnp.where(at.even == at.upward, first_ref[...], other_ref[...])
    left[:, obs : 2 * obs] = far_ref[...]
    left[:, 2 * obs :] = own_ref[...]
    points = [at.side(left, True)]
    results = point_weights(points, count, float(rows), gram, square, last, rest)
    for step in range(at.edge):
        row = at.edge_row(True, step)
        terms = [(at.share(row, at.side_point(True)), rest[0], *results[0])]
        for point in range(CP):
            small = (small_ref[point, 0:1, 0:1], small_ref[point, 8:9, :])
            terms.append((at.share(row, point), beside_ref[point], *small))
        write_mix(mix_ref, diag_ref, step, terms, count)


def weights(own, first, other, far, beyond, size, rows):
    count, obs = own.shape[0] - PAD, own.shape[1]
    edge = rows // CP // 2
    near_inputs = [own, first, other] + ([] if beyond is None else [beyond])
    mix, diag, beside, small = pl.pallas_call(
        functools.partial(near_kernel, size, rows, beyond is not None),
        out_shape=(
            pltpu.VMEM((rows, count + PAD, count), jnp.bfloat16),
            pltpu.VMEM((rows, 8, 128), jnp.float32),
            pltpu.VMEM((CP, count, count), jnp.bfloat16),
            pltpu.VMEM((CP, 16, count), jnp.float32),
        ),
        in_specs=[VMEM] * len(near_inputs),
        out_specs=(VMEM,) * 4,
        scratch_shapes=[pltpu.VMEM((count + PAD, 5 * obs), jnp.bfloat16)]
        + [pltpu.VMEM((CP + 1, count, count), jnp.bfloat16)] * 4,
        compiler_params=pltpu.CompilerParams(vmem_limit_bytes=40 * MIB),
        cost_estimate=pl.CostEstimate(
            flops=NEAR_FLOPS * count**3, bytes_accessed=8 * count * count, transcendentals=0
        ),
        name="near",
    )(*near_inputs)
    edge_mix, edge_diag = pl.pallas_call(
        functools.partial(far_kernel, size, rows),
        out_shape=(
            pltpu.VMEM((edge, count + PAD, count), jnp.bfloat16),
            pltpu.VMEM((edge, 8, 128), jnp.float32),
        ),
        in_specs=[VMEM] * 6,
        out_specs=(VMEM,) * 2,
        scratch_shapes=[pltpu.VMEM((count + PAD, 3 * obs), jnp.bfloat16)]
        + [pltpu.VMEM((1, count, count), jnp.bfloat16)] * 4,
        compiler_params=pltpu.CompilerParams(vmem_limit_bytes=32 * MIB),
        cost_estimate=pl.CostEstimate(
            flops=FAR_FLOPS * count**3, bytes_accessed=8 * count * count, transcendentals=0
        ),
        name="far",
    )(own, first, other, far, beside, small)
    return mix, diag, edge_mix, edge_diag


def analyse_kernel(size, *refs):
    mix_ref, diag_ref, edge_mix_ref, edge_diag_ref = refs[:4]
    block_refs = refs[4:-3]
    out_ref, deviations, wide = refs[-3:]
    chips = len(block_refs)
    _, rows, members, width = block_refs[0].shape
    count = 2 * chips * members
    at = Place(size, rows)
    chip = lax.axis_index("gx") // 2

    def one_row(row, mix, diag):
        halves = [(step, side) for step in range(chips) for side in range(2)]
        blocks = [block_refs[step][side, row].astype(jnp.float32) for step, side in halves]
        total = sum(jnp.sum(block, axis=0, keepdims=True) for block in blocks)
        mean = total / count
        for (step, side), block in zip(halves, blocks):
            first = (2 * source_chip(chip, step, chips) + side) * members
            deviations[pl.ds(pl.multiple_of(first, members), members), :] = (block - mean).astype(
                jnp.bfloat16
            )
        deviation = deviations[...]
        term = jnp.dot(mix, deviation, preferred_element_type=jnp.float32)
        shift = mean + term[count : count + 1] + term[count + 1 : count + 2]
        wide[pl.ds(row, count, stride=rows), :] = (
            term[0:count] + diag * deviation.astype(jnp.float32) + shift
        )

    for row in range(at.edge, rows - at.edge):
        one_row(row, mix_ref[row], diag_ref[row, 0:1, 0:width])
    for step in range(at.edge):
        row = at.edge_row(False, step)
        one_row(row, mix_ref[row], diag_ref[row, 0:1, 0:width])
    for step in range(at.edge):
        row = at.edge_row(True, step)
        one_row(row, edge_mix_ref[step], edge_diag_ref[step, 0:1, 0:width])
    out_ref[...] = wide[...].astype(jnp.bfloat16)


def analyse(blocks, mixes, size):
    _, rows, members, width = blocks[0].shape
    count = 2 * len(blocks) * members
    flat = pl.pallas_call(
        functools.partial(analyse_kernel, size),
        out_shape=jax.ShapeDtypeStruct((count * rows, width), jnp.bfloat16),
        in_specs=[VMEM] * (4 + len(blocks)),
        out_specs=VMEM,
        scratch_shapes=[
            pltpu.VMEM((count, width), jnp.bfloat16),
            pltpu.VMEM((count * rows, width), jnp.float32),
        ],
        compiler_params=pltpu.CompilerParams(vmem_limit_bytes=24 * MIB),
        name="analyse",
    )(*mixes, *blocks)
    return flat.reshape(count, rows, width)


def on_device(prior_fields, measured_spread, scaled_misfit, sensor_line_inside):
    parts = lax.axis_size("gx")
    chips = parts // 2
    size = lax.axis_size("gy")
    count = measured_spread.shape[0]
    rows = prior_fields.shape[1]
    packed, keep, give = split(
        prior_fields,
        measured_spread.reshape(count, -1),
        scaled_misfit.reshape(1, -1),
        sensor_line_inside.reshape(1, -1),
        chips,
    )

    def trade(pairs):
        return lax.ppermute(packed, "gy", pairs) if pairs else None

    got = lax.ppermute(give, "gx", [(index, index ^ 1) for index in range(parts)])
    first = trade(swap_pairs(size, 1, 0))
    other = trade(swap_pairs(size, 1, 1))
    far, beyond = trade(swap_pairs(size, 2, 0)), trade(swap_pairs(size, 2, 1))
    own, *sent = sort(keep, got)
    blocks = [own]
    for step, block in enumerate(sent, 1):
        pairs = [
            (index, 2 * target_chip(index // 2, step, chips) + index % 2) for index in range(parts)
        ]
        blocks.append(lax.ppermute(block, "gx", pairs))
    mixes = weights(packed, first, other, far, beyond, size, rows)
    return analyse(blocks, mixes, size)


def solution(mesh):
    return jax.shard_map(
        on_device,
        mesh=mesh,
        in_specs=(P("gx", "gy", None), P(None, "gy", "gx"), P("gy", "gx"), P("gy", "gx")),
        out_specs=P(None, "gy", "gx"),
        check_vma=False,
    )
```

```python
import functools

import jax
import jax.numpy as jnp
from jax import lax
from jax.experimental import pallas as pl
from jax.experimental.pallas import tpu as pltpu
from jax.sharding import PartitionSpec as P

CP = 2
PAD = 16
MIB = 1 << 20
NEAR_FLOPS = 180

VMEM = pl.BlockSpec(memory_space=pltpu.VMEM)
HBM = pl.BlockSpec(memory_space=pltpu.HBM)


def swap_pairs(size, reach, phase):
    lows = [i for i in range(size - reach) if (i // reach) % 2 == phase]
    return [pair for i in lows for pair in ((i, i + reach), (i + reach, i))]


def target_chip(chip, step, chips):
    if chips & (chips - 1) == 0:
        return chip ^ step
    return (chip + step) % chips if isinstance(chip, int) else lax.rem(chip + step, chips)


def source_chip(chip, step, chips):
    return target_chip(chip, step if chips & (chips - 1) == 0 else chips - step, chips)


def split_kernel(chips, prior_ref, spread_ref, misfit_ref, line_ref, *refs):
    packed_ref, keep_ref, give_ref, misfit, line, sems = refs
    count, width = spread_ref.shape
    copies = [
        pltpu.make_async_copy(spread_ref, packed_ref.at[0:count], sems.at[0]),
        pltpu.make_async_copy(misfit_ref, misfit, sems.at[1]),
        pltpu.make_async_copy(line_ref, line, sems.at[2]),
    ]
    core = lax.rem(lax.axis_index("gx"), 2)
    cells = prior_ref.shape[2] // (2 * chips)
    for chip in range(chips):
        for place, (side, ref) in enumerate(((core, keep_ref), (1 - core, give_ref))):
            first = pl.multiple_of((2 * chip + side) * cells, cells)
            copies.append(
                pltpu.make_async_copy(
                    prior_ref.at[:, :, pl.ds(first, cells)],
                    ref.at[chip],
                    sems.at[3 + 2 * chip + place],
                )
            )
    for copy in copies:
        copy.start()
    for copy in copies[1:3]:
        copy.wait()
    which = lax.broadcasted_iota(jnp.int32, (PAD, width), 0)
    misfits = jnp.broadcast_to(misfit[...].astype(jnp.float32), (PAD, width))
    lines = jnp.broadcast_to(line[...].astype(jnp.float32), (PAD, width))
    extra = jnp.where(which == 0, misfits, jnp.where(which == 1, lines, 0.0))
    packed_ref[count:, :] = extra.astype(jnp.bfloat16)
    copies[0].wait()
    for copy in copies[3:]:
        copy.wait()


def split(prior, spread, misfit, line, chips):
    members, rows, cells = prior.shape
    count, obs = spread.shape
    half = (chips, members, rows, cells // (2 * chips))
    inputs = (prior, spread, misfit, line)
    return pl.pallas_call(
        functools.partial(split_kernel, chips),
        out_shape=(
            pltpu.VMEM((count + PAD, obs), jnp.bfloat16),
            pltpu.VMEM(half, jnp.bfloat16),
            pltpu.VMEM(half, jnp.bfloat16),
        ),
        in_specs=[HBM] * 4,
        out_specs=(VMEM,) * 3,
        scratch_shapes=[
            pltpu.VMEM(misfit.shape, misfit.dtype),
            pltpu.VMEM(line.shape, line.dtype),
            pltpu.SemaphoreType.DMA((3 + 2 * chips,)),
        ],
        name="split",
    )(*[pltpu.with_memory_space_constraint(array, pltpu.HBM) for array in inputs])


def sort_kernel(chips, rows, keep_ref, got_ref, *refs):
    sorted_refs, wide = refs[:chips], refs[chips]
    members = keep_ref.shape[0] // (chips * rows)
    index = lax.axis_index("gx")
    core = lax.rem(index, 2)
    chip = index // 2
    for half, ref in enumerate((keep_ref, got_ref)):
        wide[half] = ref[...].astype(jnp.float32)
    for step in range(chips):
        first = target_chip(chip, step, chips) * (members * rows)
        for half, side in enumerate((core, 1 - core)):
            for row in range(rows):
                lines = wide[half, pl.ds(first + row, members, stride=rows), :]
                sorted_refs[step][side, row] = lines.astype(jnp.bfloat16)


def sort(keep, got):
    chips, members, rows, cells = keep.shape
    flat = (chips * members * rows, cells)
    return pl.pallas_call(
        functools.partial(sort_kernel, chips, rows),
        out_shape=[pltpu.VMEM((2, rows, members, cells), jnp.bfloat16)] * chips,
        in_specs=[VMEM] * 2,
        out_specs=[VMEM] * chips,
        scratch_shapes=[pltpu.VMEM((2,) + flat, jnp.float32)],
        compiler_params=pltpu.CompilerParams(vmem_limit_bytes=16 * MIB),
        cost_estimate=pl.CostEstimate(flops=0, bytes_accessed=4 * MIB, transcendentals=0),
        name="sort",
    )(keep.reshape(flat), got.reshape(flat))


def select_flag(condition):
    return jnp.where(condition, jnp.float32(1.0), jnp.float32(0.0))


class Point:
    def __init__(self, left, centre, bases, present):
        self.left, self.centre, self.bases, self.present = left, centre, bases, present


def turn(row, eye):
    block = eye.shape[0]
    pieces = [row[:, i : i + block] for i in range(0, row.shape[1], block)]
    return jnp.concatenate(
        [jnp.sum(eye * piece, axis=1, keepdims=True) for piece in pieces], axis=0
    )


def lay(column, eye):
    block = eye.shape[0]
    pieces = [column[i : i + block] for i in range(0, column.shape[0], block)]
    return jnp.concatenate(
        [jnp.sum(eye * piece, axis=0, keepdims=True) for piece in pieces], axis=1
    )


def point_weights(points, count, radius, gram_ref, square_ref, last_ref, rest_ref, between=()):
    pieces = iter(between)
    share = 1.0 / (count - 1.0)
    slots = range(len(points))
    block = min(count, 128)
    eye = jnp.where(
        lax.broadcasted_iota(jnp.int32, (block, block), 0)
        == lax.broadcasted_iota(jnp.int32, (block, block), 1),
        1.0,
        0.0,
    )
    drives, bounds = [], []
    for slot in slots:
        point = points[slot]
        left = point.left
        line = left[count + 1 : count + 2, :].astype(jnp.float32)
        obs = line.shape[1] // 3
        where = lax.broadcasted_iota(jnp.int32, line.shape, 1) // obs
        first, second, third = point.bases
        base = jnp.where(where == 0, first, jnp.where(where == 1, second, third))
        first, second, third = point.present
        alive = jnp.where(where == 0, first, jnp.where(where == 1, second, third))
        distance = (base + line + 0.5 - point.centre) / radius
        locality = jnp.exp(-0.5 * distance * distance) * alive
        scaled = (left[0:count, :].astype(jnp.float32) * locality).astype(jnp.bfloat16)
        both = lax.dot_general(
            left[...], scaled, (((1,), (1,)), ((), ())), preferred_element_type=jnp.float32
        )
        gram = both[0:count]
        drives.append(both[count : count + 1])
        gram_ref[slot] = gram.astype(jnp.bfloat16)
        sizes = jnp.sum(jnp.abs(gram), axis=0, keepdims=True)
        bounds.append(1.0 + share * jnp.max(sizes, axis=1, keepdims=True))
    next(pieces, int)()
    factors = []
    for slot in slots:
        s = 1.0 / bounds[slot]
        g = s * share
        root = lax.rsqrt(bounds[slot])
        wide = lambda value: jnp.broadcast_to(value, (1, count))
        third = wide((4.0 * s - 9.0) * (g * g) * g * (root / 16.0))
        fourth = wide((g * g) * (g * g) * (root / 16.0))
        linear = wide((-39.0 + s * (54.0 + s * (-27.0 + 4.0 * s))) * g * (root / 16.0))
        quadratic = wide((27.0 + s * (-27.0 + 6.0 * s)) * (g * g) * (root / 16.0))
        scalar_part = (36.0 + s * (-39.0 + s * (27.0 + s * (-9.0 + s)))) * (root / 16.0)
        factors.append((linear, quadratic, scalar_part, g * bounds[slot]))
        gram = gram_ref[slot]
        square = jnp.dot(gram, gram, preferred_element_type=jnp.float32)
        square_ref[slot] = square.astype(jnp.bfloat16)
        last = third * gram.astype(jnp.float32) + fourth * square
        last_ref[slot] = last.astype(jnp.bfloat16)
    next(pieces, int)()
    for slot in slots:
        linear, quadratic, scalar_part, _ = factors[slot]
        product = jnp.dot(square_ref[slot], last_ref[slot], preferred_element_type=jnp.float32)
        rest = (
            linear * gram_ref[slot].astype(jnp.float32)
            + quadratic * square_ref[slot].astype(jnp.float32)
            + product
        )
        rest_ref[slot] = rest.astype(jnp.bfloat16)

    next(pieces, int)()
    results = []
    for slot in slots:
        _, _, scalar_part, g = factors[slot]
        mean_weights = drives[slot]
        for _ in range(2):
            out = jnp.dot(two_rows(mean_weights), rest_ref[slot], preferred_element_type=jnp.float32)
            mean_weights = out[0:1] + out[1:2] + scalar_part * mean_weights
            next(pieces, int)()
        mean_weights = mean_weights * g
        results.append((scalar_part, mean_weights))
    return results


def two_rows(row):
    high = row.astype(jnp.bfloat16).astype(jnp.float32)
    which = lax.broadcasted_iota(jnp.int32, (PAD, row.shape[1]), 0)
    return jnp.where(which == 0, high, jnp.where(which == 1, row - high, 0.0)).astype(jnp.bfloat16)


class Place:
    def __init__(self, size, rows):
        self.size, self.rows = size, rows
        self.spacing = rows // CP
        self.edge = self.spacing // 2
        self.tile = lax.axis_index("gy")
        self.upward = lax.rem(self.tile // 2, 2) == 0
        self.even = lax.rem(self.tile, 2) == 0
        self.sign = jnp.where(self.upward, 1, -1)

    def present(self, offset):
        there = (self.tile + offset >= 0) & (self.tile + offset < self.size)
        return select_flag(there)

    def share(self, row, point):
        start = (self.tile * self.rows).astype(jnp.float32)
        height = float(self.rows * self.size)
        place = jnp.clip(start + row + 0.5, 0.5 * self.spacing, height - 0.5 * self.spacing)
        centre = start + (point + 0.5) * self.spacing
        return jnp.maximum(0.0, 1.0 - jnp.abs(place - centre) / self.spacing)

    def edge_row(self, ahead, step):
        first, last = step, self.rows - 1 - step
        return jnp.where(self.upward == ahead, last, first)

    def side_point(self, ahead):
        return jnp.where(self.upward == ahead, jnp.float32(CP), jnp.float32(-1))

    def own_point(self, ahead):
        return jnp.where(self.upward == ahead, jnp.float32(CP - 1), jnp.float32(0))

    def side(self, left, ahead):
        sign = self.sign if ahead else -self.sign
        offsets = (sign, 2 * sign, 0 * sign)
        centre = (self.side_point(ahead) + 0.5) * self.spacing
        return self.point(left, centre, offsets)

    def point(self, left, centre, offsets):
        bases = [(offset * self.rows).astype(jnp.float32) for offset in offsets]
        return Point(left, centre, bases, [self.present(offset) for offset in offsets])


def mix_rows(mix_ref, terms, count):
    mixed = sum(share * rest.astype(jnp.float32) for share, rest, _, _ in terms)
    mix_ref[0:count, :] = mixed.astype(jnp.bfloat16)
    mix_ref[count:, :] = two_rows(sum(share * mean for share, _, _, mean in terms))
    return sum(share * diag for share, _, diag, _ in terms)


def write_mix(mix_ref, diag_ref, row, terms, count):
    diag_ref[row] = jnp.broadcast_to(mix_rows(mix_ref.at[row], terms, count), (8, 128))


def near_kernel(size, rows, has_far, *refs):
    own_ref, first_ref, other_ref = refs[:3]
    mix_ref, diag_ref, beside_ref, small_ref, left, gram, square, last, rest = refs[
        4 if has_far else 3 :
    ]
    count, obs = own_ref.shape[0] - PAD, own_ref.shape[1]
    at = Place(size, rows)
    ahead_is_first = at.even == at.upward
    left[:, 0:obs] = jnp.where(ahead_is_first, first_ref[...], other_ref[...])
    left[:, obs : 2 * obs] = own_ref[...]
    left[:, 2 * obs : 3 * obs] = jnp.where(ahead_is_first, other_ref[...], first_ref[...])
    far = refs[3][...] if has_far else jnp.zeros(own_ref.shape, jnp.bfloat16)
    left[:, 3 * obs : 4 * obs] = far
    left[:, 4 * obs :] = own_ref[...]
    offsets = (at.sign, 0 * at.sign, -at.sign)
    points = []
    for point in range(CP):
        points.append(at.point(left.at[:, 0 : 3 * obs], (point + 0.5) * at.spacing, offsets))
    points.append(at.side(left.at[:, 2 * obs :], False))
    results = point_weights(points, count, float(rows), gram, square, last, rest)

    def term(row, point, slot):
        return (at.share(row, point), rest[slot], *results[slot])

    for row in range(at.edge, rows - at.edge):
        low = int((row + 0.5) / at.spacing - 0.5)
        terms = [term(row, low + step, low + step) for step in (0, 1)]
        write_mix(mix_ref, diag_ref, row, terms, count)
    for step in range(at.edge):
        row = at.edge_row(False, step)
        terms = [term(row, point, point) for point in range(CP)]
        terms.append(term(row, at.side_point(False), CP))
        write_mix(mix_ref, diag_ref, row, terms, count)
    for point in range(CP):
        beside_ref[point] = rest[point]
        scalar_part, mean_weights = results[point]
        small_ref[point, 0:8, :] = jnp.broadcast_to(scalar_part, (8, count))
        small_ref[point, 8:16, :] = jnp.broadcast_to(mean_weights, (8, count))


def weights(own, first, other, beyond, size, rows):
    count, obs = own.shape[0] - PAD, own.shape[1]
    near_inputs = [own, first, other] + ([] if beyond is None else [beyond])
    mix, diag, beside, small = pl.pallas_call(
        functools.partial(near_kernel, size, rows, beyond is not None),
        out_shape=(
            pltpu.VMEM((rows, count + PAD, count), jnp.bfloat16),
            pltpu.VMEM((rows, 8, 128), jnp.float32),
            pltpu.VMEM((CP, count, count), jnp.bfloat16),
            pltpu.VMEM((CP, 16, count), jnp.float32),
        ),
        in_specs=[VMEM] * len(near_inputs),
        out_specs=(VMEM,) * 4,
        scratch_shapes=[pltpu.VMEM((count + PAD, 5 * obs), jnp.bfloat16)]
        + [pltpu.VMEM((CP + 1, count, count), jnp.bfloat16)] * 4,
        compiler_params=pltpu.CompilerParams(vmem_limit_bytes=40 * MIB),
        cost_estimate=pl.CostEstimate(
            flops=NEAR_FLOPS * count**3, bytes_accessed=8 * count * count, transcendentals=0
        ),
        name="near",
    )(*near_inputs)
    return mix, diag, beside, small


def finish_kernel(size, rows, *refs):
    own_ref, first_ref, other_ref, far_ref, mix_ref, diag_ref, beside_ref, small_ref = refs[:8]
    block_refs = refs[8:-9]
    out_ref, left, gram, square, last, rest, edge_mix, deviations, wide = refs[-9:]
    chips = len(block_refs)
    _, _, members, width = block_refs[0].shape
    count, obs = own_ref.shape[0] - PAD, own_ref.shape[1]
    at = Place(size, rows)
    chip = lax.axis_index("gx") // 2
    halves = [(step, side) for step in range(chips) for side in range(2)]

    def deviate(row):
        blocks = [block_refs[step][side, row].astype(jnp.float32) for step, side in halves]
        mean = sum(jnp.sum(block, axis=0, keepdims=True) for block in blocks) / count
        for (step, side), block in zip(halves, blocks):
            first = (2 * source_chip(chip, step, chips) + side) * members
            deviations[row, pl.ds(pl.multiple_of(first, members), members), :] = (
                block - mean
            ).astype(jnp.bfloat16)
        return mean

    def apply(row, mean, mix, diag):
        deviation = deviations[row]
        term = jnp.dot(mix, deviation, preferred_element_type=jnp.float32)
        shift = mean + term[count : count + 1] + term[count + 1 : count + 2]
        wide[pl.ds(row, count, stride=rows), :] = (
            term[0:count] + diag * deviation.astype(jnp.float32) + shift
        )

    def whole_row(row):
        apply(row, deviate(row), mix_ref[row], diag_ref[row, 0:1, 0:width])

    behind = [at.edge_row(False, step) for step in range(at.edge)]
    ahead = [at.edge_row(True, step) for step in range(at.edge)]
    means = []
    between = [functools.partial(whole_row, row) for row in range(at.edge, rows - at.edge)]
    between += [functools.partial(whole_row, row) for row in behind]
    between += [lambda: means.extend([deviate(row) for row in ahead])]

    left[:, 0:obs] = jnp.where(at.even == at.upward, first_ref[...], other_ref[...])
    left[:, obs : 2 * obs] = far_ref[...]
    left[:, 2 * obs :] = own_ref[...]
    points = [at.side(left, True)]
    results = point_weights(points, count, float(rows), gram, square, last, rest, between)
    for step, row in enumerate(ahead):
        terms = [(at.share(row, at.side_point(True)), rest[0], *results[0])]
        for point in range(CP):
            small = (small_ref[point, 0:1, 0:1], small_ref[point, 8:9, :])
            terms.append((at.share(row, point), beside_ref[point], *small))
        diag = mix_rows(edge_mix.at[step], terms, count)
        apply(row, means[step], edge_mix[step], diag)
    out_ref[...] = wide[...].astype(jnp.bfloat16)


def finish(tiles, mixes, blocks, size):
    _, rows, members, width = blocks[0].shape
    count, obs = tiles[0].shape[0] - PAD, tiles[0].shape[1]
    square = pltpu.VMEM((1, count, count), jnp.bfloat16)
    flat = pl.pallas_call(
        functools.partial(finish_kernel, size, rows),
        out_shape=jax.ShapeDtypeStruct((count * rows, width), jnp.bfloat16),
        in_specs=[VMEM] * (8 + len(blocks)),
        out_specs=VMEM,
        scratch_shapes=[
            pltpu.VMEM((count + PAD, 3 * obs), jnp.bfloat16),
            square,
            square,
            square,
            square,
            pltpu.VMEM((rows // CP // 2, count + PAD, count), jnp.bfloat16),
            pltpu.VMEM((rows, count, width), jnp.bfloat16),
            pltpu.VMEM((count * rows, width), jnp.float32),
        ],
        compiler_params=pltpu.CompilerParams(vmem_limit_bytes=40 * MIB),
        name="finish",
    )(*tiles, *mixes, *blocks)
    return flat.reshape(count, rows, width)


def on_device(prior_fields, measured_spread, scaled_misfit, sensor_line_inside):
    parts = lax.axis_size("gx")
    chips = parts // 2
    size = lax.axis_size("gy")
    count = measured_spread.shape[0]
    rows = prior_fields.shape[1]
    packed, keep, give = split(
        prior_fields,
        measured_spread.reshape(count, -1),
        scaled_misfit.reshape(1, -1),
        sensor_line_inside.reshape(1, -1),
        chips,
    )

    def trade(pairs):
        return lax.ppermute(packed, "gy", pairs) if pairs else None

    got = lax.ppermute(give, "gx", [(index, index ^ 1) for index in range(parts)])
    first = trade(swap_pairs(size, 1, 0))
    other = trade(swap_pairs(size, 1, 1))
    far, beyond = trade(swap_pairs(size, 2, 0)), trade(swap_pairs(size, 2, 1))
    own, *sent = sort(keep, got)
    blocks = [own]
    for step, block in enumerate(sent, 1):
        pairs = [
            (index, 2 * target_chip(index // 2, step, chips) + index % 2) for index in range(parts)
        ]
        blocks.append(lax.ppermute(block, "gx", pairs))
    mixes = weights(packed, first, other, beyond, size, rows)
    return finish((packed, first, other, far), mixes, blocks, size)


def solution(mesh):
    return jax.shard_map(
        on_device,
        mesh=mesh,
        in_specs=(P("gx", "gy", None), P(None, "gy", "gx"), P("gy", "gx"), P("gy", "gx")),
        out_specs=P(None, "gy", "gx"),
        check_vma=False,
    )
```

```python
import functools

import jax
import jax.numpy as jnp
from jax import lax
from jax.experimental import pallas as pl
from jax.experimental.pallas import tpu as pltpu
from jax.sharding import PartitionSpec as P

CP = 2
PAD = 16
MIB = 1 << 20
NEAR_FLOPS = 180

VMEM = pl.BlockSpec(memory_space=pltpu.VMEM)
HBM = pl.BlockSpec(memory_space=pltpu.HBM)


def swap_pairs(size, reach, phase):
    lows = [i for i in range(size - reach) if (i // reach) % 2 == phase]
    return [pair for i in lows for pair in ((i, i + reach), (i + reach, i))]


def everyone(pairs, parts, size):
    idle = set(range(size)) - {place for pair in pairs for place in pair}
    moves = [(c * size + i, c * size + j) for c in range(parts) for i, j in pairs]
    return moves + [(c * size + i, (c ^ 1) * size + i) for c in range(parts) for i in sorted(idle)]


def target_chip(chip, step, chips):
    if chips & (chips - 1) == 0:
        return chip ^ step
    return (chip + step) % chips if isinstance(chip, int) else lax.rem(chip + step, chips)


def source_chip(chip, step, chips):
    return target_chip(chip, step if chips & (chips - 1) == 0 else chips - step, chips)


def split_kernel(chips, prior_ref, spread_ref, misfit_ref, line_ref, *refs):
    packed_ref, keep_ref, give_ref, misfit, line, sems = refs
    count, width = spread_ref.shape
    copies = [
        pltpu.make_async_copy(spread_ref, packed_ref.at[0:count], sems.at[0]),
        pltpu.make_async_copy(misfit_ref, misfit, sems.at[1]),
        pltpu.make_async_copy(line_ref, line, sems.at[2]),
    ]
    core = lax.rem(lax.axis_index("gx"), 2)
    cells = prior_ref.shape[2] // (2 * chips)
    for chip in range(chips):
        for place, (side, ref) in enumerate(((core, keep_ref), (1 - core, give_ref))):
            first = pl.multiple_of((2 * chip + side) * cells, cells)
            copies.append(
                pltpu.make_async_copy(
                    prior_ref.at[:, :, pl.ds(first, cells)],
                    ref.at[chip],
                    sems.at[3 + 2 * chip + place],
                )
            )
    for copy in copies:
        copy.start()
    for copy in copies[1:3]:
        copy.wait()
    which = lax.broadcasted_iota(jnp.int32, (PAD, width), 0)
    misfits = jnp.broadcast_to(misfit[...].astype(jnp.float32), (PAD, width))
    lines = jnp.broadcast_to(line[...].astype(jnp.float32), (PAD, width))
    extra = jnp.where(which == 0, misfits, jnp.where(which == 1, lines, 0.0))
    packed_ref[count:, :] = extra.astype(jnp.bfloat16)
    copies[0].wait()
    for copy in copies[3:]:
        copy.wait()


def split(prior, spread, misfit, line, chips):
    members, rows, cells = prior.shape
    count, obs = spread.shape
    half = (chips, members, rows, cells // (2 * chips))
    inputs = (prior, spread, misfit, line)
    return pl.pallas_call(
        functools.partial(split_kernel, chips),
        out_shape=(
            pltpu.VMEM((count + PAD, obs), jnp.bfloat16),
            pltpu.VMEM(half, jnp.bfloat16),
            pltpu.VMEM(half, jnp.bfloat16),
        ),
        in_specs=[HBM] * 4,
        out_specs=(VMEM,) * 3,
        scratch_shapes=[
            pltpu.VMEM(misfit.shape, misfit.dtype),
            pltpu.VMEM(line.shape, line.dtype),
            pltpu.SemaphoreType.DMA((3 + 2 * chips,)),
        ],
        name="split",
    )(*[pltpu.with_memory_space_constraint(array, pltpu.HBM) for array in inputs])


def sort_kernel(chips, rows, keep_ref, got_ref, *refs):
    sorted_refs, wide = refs[:chips], refs[chips]
    members = keep_ref.shape[0] // (chips * rows)
    index = lax.axis_index("gx")
    core = lax.rem(index, 2)
    chip = index // 2
    for half, ref in enumerate((keep_ref, got_ref)):
        wide[half] = ref[...].astype(jnp.float32)
    for step in range(chips):
        first = target_chip(chip, step, chips) * (members * rows)
        for half, side in enumerate((core, 1 - core)):
            for row in range(rows):
                lines = wide[half, pl.ds(first + row, members, stride=rows), :]
                sorted_refs[step][side, row] = lines.astype(jnp.bfloat16)


def sort(keep, got):
    chips, members, rows, cells = keep.shape
    flat = (chips * members * rows, cells)
    return pl.pallas_call(
        functools.partial(sort_kernel, chips, rows),
        out_shape=[pltpu.VMEM((2, rows, members, cells), jnp.bfloat16)] * chips,
        in_specs=[VMEM] * 2,
        out_specs=[VMEM] * chips,
        scratch_shapes=[pltpu.VMEM((2,) + flat, jnp.float32)],
        compiler_params=pltpu.CompilerParams(vmem_limit_bytes=16 * MIB),
        cost_estimate=pl.CostEstimate(flops=0, bytes_accessed=4 * MIB, transcendentals=0),
        name="sort",
    )(keep.reshape(flat), got.reshape(flat))


def select_flag(condition):
    return jnp.where(condition, jnp.float32(1.0), jnp.float32(0.0))


class Point:
    def __init__(self, left, centre, bases, present):
        self.left, self.centre, self.bases, self.present = left, centre, bases, present


def turn(row, eye):
    block = eye.shape[0]
    pieces = [row[:, i : i + block] for i in range(0, row.shape[1], block)]
    return jnp.concatenate(
        [jnp.sum(eye * piece, axis=1, keepdims=True) for piece in pieces], axis=0
    )


def lay(column, eye):
    block = eye.shape[0]
    pieces = [column[i : i + block] for i in range(0, column.shape[0], block)]
    return jnp.concatenate(
        [jnp.sum(eye * piece, axis=0, keepdims=True) for piece in pieces], axis=1
    )


def point_weights(points, count, radius, gram_ref, square_ref, last_ref, rest_ref, between=()):
    pieces = iter(between)
    share = 1.0 / (count - 1.0)
    slots = range(len(points))
    block = min(count, 128)
    eye = jnp.where(
        lax.broadcasted_iota(jnp.int32, (block, block), 0)
        == lax.broadcasted_iota(jnp.int32, (block, block), 1),
        1.0,
        0.0,
    )
    drives, bounds = [], []
    for slot in slots:
        point = points[slot]
        left = point.left
        line = left[count + 1 : count + 2, :].astype(jnp.float32)
        obs = line.shape[1] // 3
        where = lax.broadcasted_iota(jnp.int32, line.shape, 1) // obs
        first, second, third = point.bases
        base = jnp.where(where == 0, first, jnp.where(where == 1, second, third))
        first, second, third = point.present
        alive = jnp.where(where == 0, first, jnp.where(where == 1, second, third))
        distance = (base + line + 0.5 - point.centre) / radius
        locality = jnp.exp(-0.5 * distance * distance) * alive
        scaled = (left[0:count, :].astype(jnp.float32) * locality).astype(jnp.bfloat16)
        both = lax.dot_general(
            left[...], scaled, (((1,), (1,)), ((), ())), preferred_element_type=jnp.float32
        )
        gram = both[0:count]
        drives.append(both[count : count + 1])
        gram_ref[slot] = gram.astype(jnp.bfloat16)
        sizes = jnp.sum(jnp.abs(gram), axis=0, keepdims=True)
        bounds.append(1.0 + share * jnp.max(sizes, axis=1, keepdims=True))
    next(pieces, int)()
    factors = []
    for slot in slots:
        s = 1.0 / bounds[slot]
        g = s * share
        root = lax.rsqrt(bounds[slot])
        wide = lambda value: jnp.broadcast_to(value, (1, count))
        third = wide((4.0 * s - 9.0) * (g * g) * g * (root / 16.0))
        fourth = wide((g * g) * (g * g) * (root / 16.0))
        linear = wide((-39.0 + s * (54.0 + s * (-27.0 + 4.0 * s))) * g * (root / 16.0))
        quadratic = wide((27.0 + s * (-27.0 + 6.0 * s)) * (g * g) * (root / 16.0))
        scalar_part = (36.0 + s * (-39.0 + s * (27.0 + s * (-9.0 + s)))) * (root / 16.0)
        factors.append((linear, quadratic, scalar_part, g * bounds[slot]))
        gram = gram_ref[slot]
        square = jnp.dot(gram, gram, preferred_element_type=jnp.float32)
        square_ref[slot] = square.astype(jnp.bfloat16)
        last = third * gram.astype(jnp.float32) + fourth * square
        last_ref[slot] = last.astype(jnp.bfloat16)
    next(pieces, int)()
    for slot in slots:
        linear, quadratic, scalar_part, _ = factors[slot]
        product = jnp.dot(square_ref[slot], last_ref[slot], preferred_element_type=jnp.float32)
        rest = (
            linear * gram_ref[slot].astype(jnp.float32)
            + quadratic * square_ref[slot].astype(jnp.float32)
            + product
        )
        rest_ref[slot] = rest.astype(jnp.bfloat16)

    next(pieces, int)()
    results = []
    for slot in slots:
        _, _, scalar_part, g = factors[slot]
        mean_weights = drives[slot]
        for _ in range(2):
            out = jnp.dot(two_rows(mean_weights), rest_ref[slot], preferred_element_type=jnp.float32)
            mean_weights = out[0:1] + out[1:2] + scalar_part * mean_weights
            next(pieces, int)()
        mean_weights = mean_weights * g
        results.append((scalar_part, mean_weights))
    return results


def two_rows(row):
    high = row.astype(jnp.bfloat16).astype(jnp.float32)
    which = lax.broadcasted_iota(jnp.int32, (PAD, row.shape[1]), 0)
    return jnp.where(which == 0, high, jnp.where(which == 1, row - high, 0.0)).astype(jnp.bfloat16)


class Place:
    def __init__(self, size, rows):
        self.size, self.rows = size, rows
        self.spacing = rows // CP
        self.edge = self.spacing // 2
        self.tile = lax.axis_index("gy")
        self.upward = lax.rem(self.tile // 2, 2) == 0
        self.even = lax.rem(self.tile, 2) == 0
        self.sign = jnp.where(self.upward, 1, -1)

    def present(self, offset):
        there = (self.tile + offset >= 0) & (self.tile + offset < self.size)
        return select_flag(there)

    def share(self, row, point):
        start = (self.tile * self.rows).astype(jnp.float32)
        height = float(self.rows * self.size)
        place = jnp.clip(start + row + 0.5, 0.5 * self.spacing, height - 0.5 * self.spacing)
        centre = start + (point + 0.5) * self.spacing
        return jnp.maximum(0.0, 1.0 - jnp.abs(place - centre) / self.spacing)

    def edge_row(self, ahead, step):
        first, last = step, self.rows - 1 - step
        return jnp.where(self.upward == ahead, last, first)

    def side_point(self, ahead):
        return jnp.where(self.upward == ahead, jnp.float32(CP), jnp.float32(-1))

    def own_point(self, ahead):
        return jnp.where(self.upward == ahead, jnp.float32(CP - 1), jnp.float32(0))

    def side(self, left, ahead):
        sign = self.sign if ahead else -self.sign
        offsets = (sign, 2 * sign, 0 * sign)
        centre = (self.side_point(ahead) + 0.5) * self.spacing
        return self.point(left, centre, offsets)

    def point(self, left, centre, offsets):
        bases = [(offset * self.rows).astype(jnp.float32) for offset in offsets]
        return Point(left, centre, bases, [self.present(offset) for offset in offsets])


def mix_rows(mix_ref, terms, count):
    mixed = sum(share * rest.astype(jnp.float32) for share, rest, _, _ in terms)
    mix_ref[0:count, :] = mixed.astype(jnp.bfloat16)
    mix_ref[count:, :] = two_rows(sum(share * mean for share, _, _, mean in terms))
    return sum(share * diag for share, _, diag, _ in terms)


def write_mix(mix_ref, diag_ref, row, terms, count):
    diag_ref[row] = jnp.broadcast_to(mix_rows(mix_ref.at[row], terms, count), (8, 128))


def near_kernel(size, rows, has_far, *refs):
    own_ref, first_ref, other_ref = refs[:3]
    mix_ref, diag_ref, beside_ref, small_ref, left, gram, square, last, rest = refs[
        4 if has_far else 3 :
    ]
    count, obs = own_ref.shape[0] - PAD, own_ref.shape[1]
    at = Place(size, rows)
    ahead_is_first = at.even == at.upward
    left[:, 0:obs] = jnp.where(ahead_is_first, first_ref[...], other_ref[...])
    left[:, obs : 2 * obs] = own_ref[...]
    left[:, 2 * obs : 3 * obs] = jnp.where(ahead_is_first, other_ref[...], first_ref[...])
    far = refs[3][...] if has_far else jnp.zeros(own_ref.shape, jnp.bfloat16)
    left[:, 3 * obs : 4 * obs] = far
    left[:, 4 * obs :] = own_ref[...]
    offsets = (at.sign, 0 * at.sign, -at.sign)
    points = []
    for point in range(CP):
        points.append(at.point(left.at[:, 0 : 3 * obs], (point + 0.5) * at.spacing, offsets))
    points.append(at.side(left.at[:, 2 * obs :], False))
    results = point_weights(points, count, float(rows), gram, square, last, rest)

    def term(row, point, slot):
        return (at.share(row, point), rest[slot], *results[slot])

    for row in range(at.edge, rows - at.edge):
        low = int((row + 0.5) / at.spacing - 0.5)
        terms = [term(row, low + step, low + step) for step in (0, 1)]
        write_mix(mix_ref, diag_ref, row, terms, count)
    for step in range(at.edge):
        row = at.edge_row(False, step)
        terms = [term(row, point, point) for point in range(CP)]
        terms.append(term(row, at.side_point(False), CP))
        write_mix(mix_ref, diag_ref, row, terms, count)
    for point in range(CP):
        beside_ref[point] = rest[point]
        scalar_part, mean_weights = results[point]
        small_ref[point, 0:8, :] = jnp.broadcast_to(scalar_part, (8, count))
        small_ref[point, 8:16, :] = jnp.broadcast_to(mean_weights, (8, count))


def weights(own, first, other, beyond, size, rows):
    count, obs = own.shape[0] - PAD, own.shape[1]
    near_inputs = [own, first, other] + ([] if beyond is None else [beyond])
    mix, diag, beside, small = pl.pallas_call(
        functools.partial(near_kernel, size, rows, beyond is not None),
        out_shape=(
            pltpu.VMEM((rows, count + PAD, count), jnp.bfloat16),
            pltpu.VMEM((rows, 8, 128), jnp.float32),
            pltpu.VMEM((CP, count, count), jnp.bfloat16),
            pltpu.VMEM((CP, 16, count), jnp.float32),
        ),
        in_specs=[VMEM] * len(near_inputs),
        out_specs=(VMEM,) * 4,
        scratch_shapes=[pltpu.VMEM((count + PAD, 5 * obs), jnp.bfloat16)]
        + [pltpu.VMEM((CP + 1, count, count), jnp.bfloat16)] * 4,
        compiler_params=pltpu.CompilerParams(vmem_limit_bytes=40 * MIB),
        cost_estimate=pl.CostEstimate(
            flops=NEAR_FLOPS * count**3, bytes_accessed=8 * count * count, transcendentals=0
        ),
        name="near",
    )(*near_inputs)
    return mix, diag, beside, small


def finish_kernel(size, rows, *refs):
    own_ref, first_ref, other_ref, far_ref, mix_ref, diag_ref, beside_ref, small_ref = refs[:8]
    block_refs = refs[8:-9]
    out_ref, left, gram, square, last, rest, edge_mix, deviations, wide = refs[-9:]
    chips = len(block_refs)
    _, _, members, width = block_refs[0].shape
    count, obs = own_ref.shape[0] - PAD, own_ref.shape[1]
    at = Place(size, rows)
    chip = lax.axis_index("gx") // 2
    halves = [(step, side) for step in range(chips) for side in range(2)]

    def deviate(row):
        blocks = [block_refs[step][side, row].astype(jnp.float32) for step, side in halves]
        mean = sum(jnp.sum(block, axis=0, keepdims=True) for block in blocks) / count
        for (step, side), block in zip(halves, blocks):
            first = (2 * source_chip(chip, step, chips) + side) * members
            deviations[row, pl.ds(pl.multiple_of(first, members), members), :] = (
                block - mean
            ).astype(jnp.bfloat16)
        return mean

    def apply(row, mean, mix, diag):
        deviation = deviations[row]
        term = jnp.dot(mix, deviation, preferred_element_type=jnp.float32)
        shift = mean + term[count : count + 1] + term[count + 1 : count + 2]
        wide[pl.ds(row, count, stride=rows), :] = (
            term[0:count] + diag * deviation.astype(jnp.float32) + shift
        )

    def whole_row(row):
        apply(row, deviate(row), mix_ref[row], diag_ref[row, 0:1, 0:width])

    behind = [at.edge_row(False, step) for step in range(at.edge)]
    ahead = [at.edge_row(True, step) for step in range(at.edge)]
    means = []
    between = [functools.partial(whole_row, row) for row in range(at.edge, rows - at.edge)]
    between += [functools.partial(whole_row, row) for row in behind]
    between += [lambda: means.extend([deviate(row) for row in ahead])]

    left[:, 0:obs] = jnp.where(at.even == at.upward, first_ref[...], other_ref[...])
    left[:, obs : 2 * obs] = far_ref[...]
    left[:, 2 * obs :] = own_ref[...]
    points = [at.side(left, True)]
    results = point_weights(points, count, float(rows), gram, square, last, rest, between)
    for step, row in enumerate(ahead):
        terms = [(at.share(row, at.side_point(True)), rest[0], *results[0])]
        for point in range(CP):
            small = (small_ref[point, 0:1, 0:1], small_ref[point, 8:9, :])
            terms.append((at.share(row, point), beside_ref[point], *small))
        diag = mix_rows(edge_mix.at[step], terms, count)
        apply(row, means[step], edge_mix[step], diag)
    out_ref[...] = wide[...].astype(jnp.bfloat16)


def finish(tiles, mixes, blocks, size):
    _, rows, members, width = blocks[0].shape
    count, obs = tiles[0].shape[0] - PAD, tiles[0].shape[1]
    square = pltpu.VMEM((1, count, count), jnp.bfloat16)
    flat = pl.pallas_call(
        functools.partial(finish_kernel, size, rows),
        out_shape=jax.ShapeDtypeStruct((count * rows, width), jnp.bfloat16),
        in_specs=[VMEM] * (8 + len(blocks)),
        out_specs=VMEM,
        scratch_shapes=[
            pltpu.VMEM((count + PAD, 3 * obs), jnp.bfloat16),
            square,
            square,
            square,
            square,
            pltpu.VMEM((rows // CP // 2, count + PAD, count), jnp.bfloat16),
            pltpu.VMEM((rows, count, width), jnp.bfloat16),
            pltpu.VMEM((count * rows, width), jnp.float32),
        ],
        compiler_params=pltpu.CompilerParams(vmem_limit_bytes=40 * MIB),
        name="finish",
    )(*tiles, *mixes, *blocks)
    return flat.reshape(count, rows, width)


def on_device(prior_fields, measured_spread, scaled_misfit, sensor_line_inside):
    parts = lax.axis_size("gx")
    chips = parts // 2
    size = lax.axis_size("gy")
    count = measured_spread.shape[0]
    rows = prior_fields.shape[1]
    packed, keep, give = split(
        prior_fields,
        measured_spread.reshape(count, -1),
        scaled_misfit.reshape(1, -1),
        sensor_line_inside.reshape(1, -1),
        chips,
    )

    def trade(pairs):
        if not pairs:
            return None
        return lax.ppermute(packed, ("gx", "gy"), everyone(pairs, parts, size))

    got = lax.ppermute(give, "gx", [(index, index ^ 1) for index in range(parts)])
    first = trade(swap_pairs(size, 1, 0))
    other = trade(swap_pairs(size, 1, 1))
    far, beyond = trade(swap_pairs(size, 2, 0)), trade(swap_pairs(size, 2, 1))
    own, *sent = sort(keep, got)
    blocks = [own]
    for step, block in enumerate(sent, 1):
        pairs = [
            (index, 2 * target_chip(index // 2, step, chips) + index % 2) for index in range(parts)
        ]
        blocks.append(lax.ppermute(block, "gx", pairs))
    mixes = weights(packed, first, other, beyond, size, rows)
    return finish((packed, first, other, far), mixes, blocks, size)


def solution(mesh):
    return jax.shard_map(
        on_device,
        mesh=mesh,
        in_specs=(P("gx", "gy", None), P(None, "gy", "gx"), P("gy", "gx"), P("gy", "gx")),
        out_specs=P(None, "gy", "gx"),
        check_vma=False,
    )
```

```python
import functools

import jax
import jax.numpy as jnp
from jax import lax
from jax.experimental import pallas as pl
from jax.experimental.pallas import tpu as pltpu
from jax.sharding import PartitionSpec as P

CP = 2
PAD = 16
MIB = 1 << 20
NEAR_FLOPS = 180

VMEM = pl.BlockSpec(memory_space=pltpu.VMEM)
HBM = pl.BlockSpec(memory_space=pltpu.HBM)


def swap_pairs(size, reach, phase):
    lows = [i for i in range(size - reach) if (i // reach) % 2 == phase]
    return [pair for i in lows for pair in ((i, i + reach), (i + reach, i))]


def everyone(pairs, parts, size):
    idle = set(range(size)) - {place for pair in pairs for place in pair}
    moves = [(c * size + i, c * size + j) for c in range(parts) for i, j in pairs]
    return moves + [(c * size + i, (c ^ 1) * size + i) for c in range(parts) for i in sorted(idle)]


def target_chip(chip, step, chips):
    if chips & (chips - 1) == 0:
        return chip ^ step
    return (chip + step) % chips if isinstance(chip, int) else lax.rem(chip + step, chips)


def exchange_steps(chips):
    return [0] + sorted(range(1, chips), key=lambda step: -step.bit_count())


def source_chip(chip, step, chips):
    return target_chip(chip, step if chips & (chips - 1) == 0 else chips - step, chips)


def split_kernel(chips, prior_ref, spread_ref, misfit_ref, line_ref, *refs):
    packed_ref, keep_ref, give_ref, misfit, line, sems = refs
    count, width = spread_ref.shape
    copies = [
        pltpu.make_async_copy(spread_ref, packed_ref.at[0:count], sems.at[0]),
        pltpu.make_async_copy(misfit_ref, misfit, sems.at[1]),
        pltpu.make_async_copy(line_ref, line, sems.at[2]),
    ]
    core = lax.rem(lax.axis_index("gx"), 2)
    cells = prior_ref.shape[2] // (2 * chips)
    for chip in range(chips):
        for place, (side, ref) in enumerate(((core, keep_ref), (1 - core, give_ref))):
            first = pl.multiple_of((2 * chip + side) * cells, cells)
            copies.append(
                pltpu.make_async_copy(
                    prior_ref.at[:, :, pl.ds(first, cells)],
                    ref.at[chip],
                    sems.at[3 + 2 * chip + place],
                )
            )
    for copy in copies:
        copy.start()
    for copy in copies[1:3]:
        copy.wait()
    which = lax.broadcasted_iota(jnp.int32, (PAD, width), 0)
    misfits = jnp.broadcast_to(misfit[...].astype(jnp.float32), (PAD, width))
    lines = jnp.broadcast_to(line[...].astype(jnp.float32), (PAD, width))
    extra = jnp.where(which == 0, misfits, jnp.where(which == 1, lines, 0.0))
    packed_ref[count:, :] = extra.astype(jnp.bfloat16)
    copies[0].wait()
    for copy in copies[3:]:
        copy.wait()


def split(prior, spread, misfit, line, chips):
    members, rows, cells = prior.shape
    count, obs = spread.shape
    half = (chips, members, rows, cells // (2 * chips))
    inputs = (prior, spread, misfit, line)
    return pl.pallas_call(
        functools.partial(split_kernel, chips),
        out_shape=(
            pltpu.VMEM((count + PAD, obs), jnp.bfloat16),
            pltpu.VMEM(half, jnp.bfloat16),
            pltpu.VMEM(half, jnp.bfloat16),
        ),
        in_specs=[HBM] * 4,
        out_specs=(VMEM,) * 3,
        scratch_shapes=[
            pltpu.VMEM(misfit.shape, misfit.dtype),
            pltpu.VMEM(line.shape, line.dtype),
            pltpu.SemaphoreType.DMA((3 + 2 * chips,)),
        ],
        name="split",
    )(*[pltpu.with_memory_space_constraint(array, pltpu.HBM) for array in inputs])


def sort_kernel(chips, rows, keep_ref, got_ref, *refs):
    sorted_refs, wide = refs[:chips], refs[chips]
    members = keep_ref.shape[0] // (chips * rows)
    index = lax.axis_index("gx")
    core = lax.rem(index, 2)
    chip = index // 2
    for half, ref in enumerate((keep_ref, got_ref)):
        wide[half] = ref[...].astype(jnp.float32)
    for step in range(chips):
        first = target_chip(chip, step, chips) * (members * rows)
        for half, side in enumerate((core, 1 - core)):
            for row in range(rows):
                lines = wide[half, pl.ds(first + row, members, stride=rows), :]
                sorted_refs[step][side, row] = lines.astype(jnp.bfloat16)


def sort(keep, got):
    chips, members, rows, cells = keep.shape
    flat = (chips * members * rows, cells)
    return pl.pallas_call(
        functools.partial(sort_kernel, chips, rows),
        out_shape=[pltpu.VMEM((2, rows, members, cells), jnp.bfloat16)] * chips,
        in_specs=[VMEM] * 2,
        out_specs=[VMEM] * chips,
        scratch_shapes=[pltpu.VMEM((2,) + flat, jnp.float32)],
        compiler_params=pltpu.CompilerParams(vmem_limit_bytes=16 * MIB),
        cost_estimate=pl.CostEstimate(flops=0, bytes_accessed=4 * MIB, transcendentals=0),
        name="sort",
    )(keep.reshape(flat), got.reshape(flat))


def select_flag(condition):
    return jnp.where(condition, jnp.float32(1.0), jnp.float32(0.0))


class Point:
    def __init__(self, left, centre, bases, present):
        self.left, self.centre, self.bases, self.present = left, centre, bases, present


def turn(row, eye):
    block = eye.shape[0]
    pieces = [row[:, i : i + block] for i in range(0, row.shape[1], block)]
    return jnp.concatenate(
        [jnp.sum(eye * piece, axis=1, keepdims=True) for piece in pieces], axis=0
    )


def lay(column, eye):
    block = eye.shape[0]
    pieces = [column[i : i + block] for i in range(0, column.shape[0], block)]
    return jnp.concatenate(
        [jnp.sum(eye * piece, axis=0, keepdims=True) for piece in pieces], axis=1
    )


def point_weights(points, count, radius, gram_ref, square_ref, last_ref, rest_ref, between=()):
    pieces = iter(between)
    share = 1.0 / (count - 1.0)
    slots = range(len(points))
    block = min(count, 128)
    eye = jnp.where(
        lax.broadcasted_iota(jnp.int32, (block, block), 0)
        == lax.broadcasted_iota(jnp.int32, (block, block), 1),
        1.0,
        0.0,
    )
    drives, bounds = [], []
    for slot in slots:
        point = points[slot]
        left = point.left
        line = left[count + 1 : count + 2, :].astype(jnp.float32)
        obs = line.shape[1] // 3
        where = lax.broadcasted_iota(jnp.int32, line.shape, 1) // obs
        first, second, third = point.bases
        base = jnp.where(where == 0, first, jnp.where(where == 1, second, third))
        first, second, third = point.present
        alive = jnp.where(where == 0, first, jnp.where(where == 1, second, third))
        distance = (base + line + 0.5 - point.centre) / radius
        locality = jnp.exp(-0.5 * distance * distance) * alive
        scaled = (left[0:count, :].astype(jnp.float32) * locality).astype(jnp.bfloat16)
        both = lax.dot_general(
            left[...], scaled, (((1,), (1,)), ((), ())), preferred_element_type=jnp.float32
        )
        gram = both[0:count]
        drives.append(both[count : count + 1])
        gram_ref[slot] = gram.astype(jnp.bfloat16)
        sizes = jnp.sum(jnp.abs(gram), axis=0, keepdims=True)
        bounds.append(1.0 + share * jnp.max(sizes, axis=1, keepdims=True))
    next(pieces, int)()
    factors = []
    for slot in slots:
        s = 1.0 / bounds[slot]
        g = s * share
        root = lax.rsqrt(bounds[slot])
        wide = lambda value: jnp.broadcast_to(value, (1, count))
        third = wide((4.0 * s - 9.0) * (g * g) * g * (root / 16.0))
        fourth = wide((g * g) * (g * g) * (root / 16.0))
        linear = wide((-39.0 + s * (54.0 + s * (-27.0 + 4.0 * s))) * g * (root / 16.0))
        quadratic = wide((27.0 + s * (-27.0 + 6.0 * s)) * (g * g) * (root / 16.0))
        scalar_part = (36.0 + s * (-39.0 + s * (27.0 + s * (-9.0 + s)))) * (root / 16.0)
        factors.append((linear, quadratic, scalar_part, g * bounds[slot]))
        gram = gram_ref[slot]
        square = jnp.dot(gram, gram, preferred_element_type=jnp.float32)
        square_ref[slot] = square.astype(jnp.bfloat16)
        last = third * gram.astype(jnp.float32) + fourth * square
        last_ref[slot] = last.astype(jnp.bfloat16)
    next(pieces, int)()
    for slot in slots:
        linear, quadratic, scalar_part, _ = factors[slot]
        product = jnp.dot(square_ref[slot], last_ref[slot], preferred_element_type=jnp.float32)
        rest = (
            linear * gram_ref[slot].astype(jnp.float32)
            + quadratic * square_ref[slot].astype(jnp.float32)
            + product
        )
        rest_ref[slot] = rest.astype(jnp.bfloat16)

    next(pieces, int)()
    results = []
    for slot in slots:
        _, _, scalar_part, g = factors[slot]
        mean_weights = drives[slot]
        for _ in range(2):
            out = jnp.dot(two_rows(mean_weights), rest_ref[slot], preferred_element_type=jnp.float32)
            mean_weights = out[0:1] + out[1:2] + scalar_part * mean_weights
            next(pieces, int)()
        mean_weights = mean_weights * g
        results.append((scalar_part, mean_weights))
    return results


def two_rows(row):
    high = row.astype(jnp.bfloat16).astype(jnp.float32)
    which = lax.broadcasted_iota(jnp.int32, (PAD, row.shape[1]), 0)
    return jnp.where(which == 0, high, jnp.where(which == 1, row - high, 0.0)).astype(jnp.bfloat16)


class Place:
    def __init__(self, size, rows):
        self.size, self.rows = size, rows
        self.spacing = rows // CP
        self.edge = self.spacing // 2
        self.tile = lax.axis_index("gy")
        self.upward = lax.rem(self.tile // 2, 2) == 0
        self.even = lax.rem(self.tile, 2) == 0
        self.sign = jnp.where(self.upward, 1, -1)

    def present(self, offset):
        there = (self.tile + offset >= 0) & (self.tile + offset < self.size)
        return select_flag(there)

    def share(self, row, point):
        start = (self.tile * self.rows).astype(jnp.float32)
        height = float(self.rows * self.size)
        place = jnp.clip(start + row + 0.5, 0.5 * self.spacing, height - 0.5 * self.spacing)
        centre = start + (point + 0.5) * self.spacing
        return jnp.maximum(0.0, 1.0 - jnp.abs(place - centre) / self.spacing)

    def edge_row(self, ahead, step):
        first, last = step, self.rows - 1 - step
        return jnp.where(self.upward == ahead, last, first)

    def side_point(self, ahead):
        return jnp.where(self.upward == ahead, jnp.float32(CP), jnp.float32(-1))

    def own_point(self, ahead):
        return jnp.where(self.upward == ahead, jnp.float32(CP - 1), jnp.float32(0))

    def side(self, left, ahead):
        sign = self.sign if ahead else -self.sign
        offsets = (sign, 2 * sign, 0 * sign)
        centre = (self.side_point(ahead) + 0.5) * self.spacing
        return self.point(left, centre, offsets)

    def point(self, left, centre, offsets):
        bases = [(offset * self.rows).astype(jnp.float32) for offset in offsets]
        return Point(left, centre, bases, [self.present(offset) for offset in offsets])


def mix_rows(mix_ref, terms, count):
    mixed = sum(share * rest.astype(jnp.float32) for share, rest, _, _ in terms)
    mix_ref[0:count, :] = mixed.astype(jnp.bfloat16)
    mix_ref[count:, :] = two_rows(sum(share * mean for share, _, _, mean in terms))
    return sum(share * diag for share, _, diag, _ in terms)


def write_mix(mix_ref, diag_ref, row, terms, count):
    diag_ref[row] = jnp.broadcast_to(mix_rows(mix_ref.at[row], terms, count), (8, 128))


def near_kernel(size, rows, has_far, *refs):
    own_ref, first_ref, other_ref = refs[:3]
    mix_ref, diag_ref, beside_ref, small_ref, left, gram, square, last, rest = refs[
        4 if has_far else 3 :
    ]
    count, obs = own_ref.shape[0] - PAD, own_ref.shape[1]
    at = Place(size, rows)
    ahead_is_first = at.even == at.upward
    left[:, 0:obs] = jnp.where(ahead_is_first, first_ref[...], other_ref[...])
    left[:, obs : 2 * obs] = own_ref[...]
    left[:, 2 * obs : 3 * obs] = jnp.where(ahead_is_first, other_ref[...], first_ref[...])
    far = refs[3][...] if has_far else jnp.zeros(own_ref.shape, jnp.bfloat16)
    left[:, 3 * obs : 4 * obs] = far
    left[:, 4 * obs :] = own_ref[...]
    offsets = (at.sign, 0 * at.sign, -at.sign)
    points = []
    for point in range(CP):
        points.append(at.point(left.at[:, 0 : 3 * obs], (point + 0.5) * at.spacing, offsets))
    points.append(at.side(left.at[:, 2 * obs :], False))
    results = point_weights(points, count, float(rows), gram, square, last, rest)

    def term(row, point, slot):
        return (at.share(row, point), rest[slot], *results[slot])

    for row in range(at.edge, rows - at.edge):
        low = int((row + 0.5) / at.spacing - 0.5)
        terms = [term(row, low + step, low + step) for step in (0, 1)]
        write_mix(mix_ref, diag_ref, row, terms, count)
    for step in range(at.edge):
        row = at.edge_row(False, step)
        terms = [term(row, point, point) for point in range(CP)]
        terms.append(term(row, at.side_point(False), CP))
        write_mix(mix_ref, diag_ref, row, terms, count)
    for point in range(CP):
        beside_ref[point] = rest[point]
        scalar_part, mean_weights = results[point]
        small_ref[point, 0:8, :] = jnp.broadcast_to(scalar_part, (8, count))
        small_ref[point, 8:16, :] = jnp.broadcast_to(mean_weights, (8, count))


def weights(own, first, other, beyond, size, rows):
    count, obs = own.shape[0] - PAD, own.shape[1]
    near_inputs = [own, first, other] + ([] if beyond is None else [beyond])
    mix, diag, beside, small = pl.pallas_call(
        functools.partial(near_kernel, size, rows, beyond is not None),
        out_shape=(
            pltpu.VMEM((rows, count + PAD, count), jnp.bfloat16),
            pltpu.VMEM((rows, 8, 128), jnp.float32),
            pltpu.VMEM((CP, count, count), jnp.bfloat16),
            pltpu.VMEM((CP, 16, count), jnp.float32),
        ),
        in_specs=[VMEM] * len(near_inputs),
        out_specs=(VMEM,) * 4,
        scratch_shapes=[pltpu.VMEM((count + PAD, 5 * obs), jnp.bfloat16)]
        + [pltpu.VMEM((CP + 1, count, count), jnp.bfloat16)] * 4,
        compiler_params=pltpu.CompilerParams(vmem_limit_bytes=40 * MIB),
        cost_estimate=pl.CostEstimate(
            flops=NEAR_FLOPS * count**3, bytes_accessed=8 * count * count, transcendentals=0
        ),
        name="near",
    )(*near_inputs)
    return mix, diag, beside, small


def finish_kernel(size, rows, *refs):
    own_ref, first_ref, other_ref, far_ref, mix_ref, diag_ref, beside_ref, small_ref = refs[:8]
    block_refs = refs[8:-9]
    out_ref, left, gram, square, last, rest, edge_mix, deviations, wide = refs[-9:]
    chips = len(block_refs)
    _, _, members, width = block_refs[0].shape
    count, obs = own_ref.shape[0] - PAD, own_ref.shape[1]
    at = Place(size, rows)
    chip = lax.axis_index("gx") // 2
    steps = exchange_steps(chips)
    halves = [(place, step, side) for place, step in enumerate(steps) for side in range(2)]

    def deviate(row):
        blocks = [block_refs[place][side, row].astype(jnp.float32) for place, _, side in halves]
        mean = sum(jnp.sum(block, axis=0, keepdims=True) for block in blocks) / count
        for (_, step, side), block in zip(halves, blocks):
            first = (2 * source_chip(chip, step, chips) + side) * members
            deviations[row, pl.ds(pl.multiple_of(first, members), members), :] = (
                block - mean
            ).astype(jnp.bfloat16)
        return mean

    def apply(row, mean, mix, diag):
        deviation = deviations[row]
        term = jnp.dot(mix, deviation, preferred_element_type=jnp.float32)
        shift = mean + term[count : count + 1] + term[count + 1 : count + 2]
        wide[pl.ds(row, count, stride=rows), :] = (
            term[0:count] + diag * deviation.astype(jnp.float32) + shift
        )

    def whole_row(row):
        apply(row, deviate(row), mix_ref[row], diag_ref[row, 0:1, 0:width])

    behind = [at.edge_row(False, step) for step in range(at.edge)]
    ahead = [at.edge_row(True, step) for step in range(at.edge)]
    means = []
    between = [functools.partial(whole_row, row) for row in range(at.edge, rows - at.edge)]
    between += [functools.partial(whole_row, row) for row in behind]
    between += [lambda: means.extend([deviate(row) for row in ahead])]

    left[:, 0:obs] = jnp.where(at.even == at.upward, first_ref[...], other_ref[...])
    left[:, obs : 2 * obs] = far_ref[...]
    left[:, 2 * obs :] = own_ref[...]
    points = [at.side(left, True)]
    results = point_weights(points, count, float(rows), gram, square, last, rest, between)
    for step, row in enumerate(ahead):
        terms = [(at.share(row, at.side_point(True)), rest[0], *results[0])]
        for point in range(CP):
            small = (small_ref[point, 0:1, 0:1], small_ref[point, 8:9, :])
            terms.append((at.share(row, point), beside_ref[point], *small))
        diag = mix_rows(edge_mix.at[step], terms, count)
        apply(row, means[step], edge_mix[step], diag)
    out_ref[...] = wide[...].astype(jnp.bfloat16)


def finish(tiles, mixes, blocks, size):
    _, rows, members, width = blocks[0].shape
    count, obs = tiles[0].shape[0] - PAD, tiles[0].shape[1]
    square = pltpu.VMEM((1, count, count), jnp.bfloat16)
    flat = pl.pallas_call(
        functools.partial(finish_kernel, size, rows),
        out_shape=jax.ShapeDtypeStruct((count * rows, width), jnp.bfloat16),
        in_specs=[VMEM] * (8 + len(blocks)),
        out_specs=VMEM,
        scratch_shapes=[
            pltpu.VMEM((count + PAD, 3 * obs), jnp.bfloat16),
            square,
            square,
            square,
            square,
            pltpu.VMEM((rows // CP // 2, count + PAD, count), jnp.bfloat16),
            pltpu.VMEM((rows, count, width), jnp.bfloat16),
            pltpu.VMEM((count * rows, width), jnp.float32),
        ],
        compiler_params=pltpu.CompilerParams(vmem_limit_bytes=40 * MIB),
        name="finish",
    )(*tiles, *mixes, *blocks)
    return flat.reshape(count, rows, width)


def on_device(prior_fields, measured_spread, scaled_misfit, sensor_line_inside):
    parts = lax.axis_size("gx")
    chips = parts // 2
    size = lax.axis_size("gy")
    count = measured_spread.shape[0]
    rows = prior_fields.shape[1]
    packed, keep, give = split(
        prior_fields,
        measured_spread.reshape(count, -1),
        scaled_misfit.reshape(1, -1),
        sensor_line_inside.reshape(1, -1),
        chips,
    )

    def trade(pairs):
        if not pairs:
            return None
        return lax.ppermute(packed, ("gx", "gy"), everyone(pairs, parts, size))

    got = lax.ppermute(give, "gx", [(index, index ^ 1) for index in range(parts)])
    first = trade(swap_pairs(size, 1, 0))
    other = trade(swap_pairs(size, 1, 1))
    far, beyond = trade(swap_pairs(size, 2, 0)), trade(swap_pairs(size, 2, 1))
    own_blocks = sort(keep, got)
    blocks = [own_blocks[0]]
    for step in exchange_steps(chips)[1:]:
        pairs = [
            (index, 2 * target_chip(index // 2, step, chips) + index % 2) for index in range(parts)
        ]
        blocks.append(lax.ppermute(own_blocks[step], "gx", pairs))
    mixes = weights(packed, first, other, beyond, size, rows)
    return finish((packed, first, other, far), mixes, blocks, size)


def solution(mesh):
    return jax.shard_map(
        on_device,
        mesh=mesh,
        in_specs=(P("gx", "gy", None), P(None, "gy", "gx"), P("gy", "gx"), P("gy", "gx")),
        out_specs=P(None, "gy", "gx"),
        check_vma=False,
    )
```

```python
import functools

import jax
import jax.numpy as jnp
from jax import lax
from jax.experimental import pallas as pl
from jax.experimental.pallas import tpu as pltpu
from jax.sharding import PartitionSpec as P

CP = 2
PAD = 16
MIB = 1 << 20
NEAR_FLOPS = 180

VMEM = pl.BlockSpec(memory_space=pltpu.VMEM)
HBM = pl.BlockSpec(memory_space=pltpu.HBM)


def swap_pairs(size, reach, phase):
    lows = [i for i in range(size - reach) if (i // reach) % 2 == phase]
    return [pair for i in lows for pair in ((i, i + reach), (i + reach, i))]


def everyone(pairs, parts, size):
    idle = set(range(size)) - {place for pair in pairs for place in pair}
    moves = [(c * size + i, c * size + j) for c in range(parts) for i, j in pairs]
    return moves + [(c * size + i, (c ^ 1) * size + i) for c in range(parts) for i in sorted(idle)]


def target_chip(chip, step, chips):
    if chips & (chips - 1) == 0:
        return chip ^ step
    return (chip + step) % chips if isinstance(chip, int) else lax.rem(chip + step, chips)


def exchange_steps(chips):
    return [0] + sorted(range(1, chips), key=lambda step: -step.bit_count())


def source_chip(chip, step, chips):
    return target_chip(chip, step if chips & (chips - 1) == 0 else chips - step, chips)


def split_kernel(chips, prior_ref, spread_ref, misfit_ref, line_ref, *refs):
    packed_ref, keep_ref, give_ref, misfit, line, sems = refs
    count, width = spread_ref.shape
    copies = [
        pltpu.make_async_copy(spread_ref, packed_ref.at[0:count], sems.at[0]),
        pltpu.make_async_copy(misfit_ref, misfit, sems.at[1]),
        pltpu.make_async_copy(line_ref, line, sems.at[2]),
    ]
    core = lax.rem(lax.axis_index("gx"), 2)
    cells = prior_ref.shape[2] // (2 * chips)
    for chip in range(chips):
        for place, (side, ref) in enumerate(((core, keep_ref), (1 - core, give_ref))):
            first = pl.multiple_of((2 * chip + side) * cells, cells)
            copies.append(
                pltpu.make_async_copy(
                    prior_ref.at[:, :, pl.ds(first, cells)],
                    ref.at[chip],
                    sems.at[3 + 2 * chip + place],
                )
            )
    for copy in copies:
        copy.start()
    for copy in copies[1:3]:
        copy.wait()
    which = lax.broadcasted_iota(jnp.int32, (PAD, width), 0)
    misfits = jnp.broadcast_to(misfit[...].astype(jnp.float32), (PAD, width))
    lines = jnp.broadcast_to(line[...].astype(jnp.float32), (PAD, width))
    extra = jnp.where(which == 0, misfits, jnp.where(which == 1, lines, 0.0))
    packed_ref[count:, :] = extra.astype(jnp.bfloat16)
    copies[0].wait()
    for copy in copies[3:]:
        copy.wait()


def split(prior, spread, misfit, line, chips):
    members, rows, cells = prior.shape
    count, obs = spread.shape
    half = (chips, members, rows, cells // (2 * chips))
    inputs = (prior, spread, misfit, line)
    return pl.pallas_call(
        functools.partial(split_kernel, chips),
        out_shape=(
            pltpu.VMEM((count + PAD, obs), jnp.bfloat16),
            pltpu.VMEM(half, jnp.bfloat16),
            pltpu.VMEM(half, jnp.bfloat16),
        ),
        in_specs=[HBM] * 4,
        out_specs=(VMEM,) * 3,
        scratch_shapes=[
            pltpu.VMEM(misfit.shape, misfit.dtype),
            pltpu.VMEM(line.shape, line.dtype),
            pltpu.SemaphoreType.DMA((3 + 2 * chips,)),
        ],
        name="split",
    )(*[pltpu.with_memory_space_constraint(array, pltpu.HBM) for array in inputs])


def sort_kernel(chips, rows, keep_ref, got_ref, *refs):
    sorted_refs, wide = refs[:chips], refs[chips]
    members = keep_ref.shape[0] // (chips * rows)
    index = lax.axis_index("gx")
    core = lax.rem(index, 2)
    chip = index // 2
    for half, ref in enumerate((keep_ref, got_ref)):
        wide[half] = ref[...].astype(jnp.float32)
    for step in range(chips):
        first = target_chip(chip, step, chips) * (members * rows)
        for half, side in enumerate((core, 1 - core)):
            for row in range(rows):
                lines = wide[half, pl.ds(first + row, members, stride=rows), :]
                sorted_refs[step][side, row] = lines.astype(jnp.bfloat16)


def sort(keep, got):
    chips, members, rows, cells = keep.shape
    flat = (chips * members * rows, cells)
    return pl.pallas_call(
        functools.partial(sort_kernel, chips, rows),
        out_shape=[pltpu.VMEM((2, rows, members, cells), jnp.bfloat16)] * chips,
        in_specs=[VMEM] * 2,
        out_specs=[VMEM] * chips,
        scratch_shapes=[pltpu.VMEM((2,) + flat, jnp.float32)],
        compiler_params=pltpu.CompilerParams(vmem_limit_bytes=16 * MIB),
        cost_estimate=pl.CostEstimate(flops=0, bytes_accessed=4 * MIB, transcendentals=0),
        name="sort",
    )(keep.reshape(flat), got.reshape(flat))


def select_flag(condition):
    return jnp.where(condition, jnp.float32(1.0), jnp.float32(0.0))


class Point:
    def __init__(self, left, centre, bases, present):
        self.left, self.centre, self.bases, self.present = left, centre, bases, present


def turn(row, eye):
    block = eye.shape[0]
    pieces = [row[:, i : i + block] for i in range(0, row.shape[1], block)]
    return jnp.concatenate(
        [jnp.sum(eye * piece, axis=1, keepdims=True) for piece in pieces], axis=0
    )


def lay(column, eye):
    block = eye.shape[0]
    pieces = [column[i : i + block] for i in range(0, column.shape[0], block)]
    return jnp.concatenate(
        [jnp.sum(eye * piece, axis=0, keepdims=True) for piece in pieces], axis=1
    )


def point_weights(points, count, radius, gram_ref, square_ref, last_ref, rest_ref, between=()):
    pieces = iter(between)
    share = 1.0 / (count - 1.0)
    slots = range(len(points))
    block = min(count, 128)
    eye = jnp.where(
        lax.broadcasted_iota(jnp.int32, (block, block), 0)
        == lax.broadcasted_iota(jnp.int32, (block, block), 1),
        1.0,
        0.0,
    )
    drives, bounds = [], []
    for slot in slots:
        point = points[slot]
        left = point.left
        line = left[count + 1 : count + 2, :].astype(jnp.float32)
        obs = line.shape[1] // 3
        where = lax.broadcasted_iota(jnp.int32, line.shape, 1) // obs
        first, second, third = point.bases
        base = jnp.where(where == 0, first, jnp.where(where == 1, second, third))
        first, second, third = point.present
        alive = jnp.where(where == 0, first, jnp.where(where == 1, second, third))
        distance = (base + line + 0.5 - point.centre) / radius
        locality = jnp.exp(-0.5 * distance * distance) * alive
        scaled = (left[0:count, :].astype(jnp.float32) * locality).astype(jnp.bfloat16)
        both = lax.dot_general(
            left[...], scaled, (((1,), (1,)), ((), ())), preferred_element_type=jnp.float32
        )
        gram = both[0:count]
        drives.append(both[count : count + 1])
        gram_ref[slot] = gram.astype(jnp.bfloat16)
        sizes = jnp.sum(jnp.abs(gram), axis=0, keepdims=True)
        bounds.append(1.0 + share * jnp.max(sizes, axis=1, keepdims=True))
    next(pieces, int)()
    factors = []
    for slot in slots:
        s = 1.0 / bounds[slot]
        g = s * share
        root = lax.rsqrt(bounds[slot])
        wide = lambda value: jnp.broadcast_to(value, (1, count))
        third = wide((4.0 * s - 9.0) * (g * g) * g * (root / 16.0))
        fourth = wide((g * g) * (g * g) * (root / 16.0))
        linear = wide((-39.0 + s * (54.0 + s * (-27.0 + 4.0 * s))) * g * (root / 16.0))
        quadratic = wide((27.0 + s * (-27.0 + 6.0 * s)) * (g * g) * (root / 16.0))
        scalar_part = (36.0 + s * (-39.0 + s * (27.0 + s * (-9.0 + s)))) * (root / 16.0)
        factors.append((linear, quadratic, scalar_part, g * bounds[slot]))
        gram = gram_ref[slot]
        square = jnp.dot(gram, gram, preferred_element_type=jnp.float32)
        square_ref[slot] = square.astype(jnp.bfloat16)
        last = third * gram.astype(jnp.float32) + fourth * square
        last_ref[slot] = last.astype(jnp.bfloat16)
    next(pieces, int)()
    for slot in slots:
        linear, quadratic, scalar_part, _ = factors[slot]
        product = jnp.dot(square_ref[slot], last_ref[slot], preferred_element_type=jnp.float32)
        rest = (
            linear * gram_ref[slot].astype(jnp.float32)
            + quadratic * square_ref[slot].astype(jnp.float32)
            + product
        )
        rest_ref[slot] = rest.astype(jnp.bfloat16)

    next(pieces, int)()
    results = []
    for slot in slots:
        _, _, scalar_part, g = factors[slot]
        mean_weights = drives[slot]
        for _ in range(2):
            out = jnp.dot(two_rows(mean_weights), rest_ref[slot], preferred_element_type=jnp.float32)
            mean_weights = out[0:1] + out[1:2] + scalar_part * mean_weights
            next(pieces, int)()
        mean_weights = mean_weights * g
        results.append((scalar_part, mean_weights))
    return results


def two_rows(row):
    high = row.astype(jnp.bfloat16).astype(jnp.float32)
    which = lax.broadcasted_iota(jnp.int32, (PAD, row.shape[1]), 0)
    return jnp.where(which == 0, high, jnp.where(which == 1, row - high, 0.0)).astype(jnp.bfloat16)


class Place:
    def __init__(self, size, rows):
        self.size, self.rows = size, rows
        self.spacing = rows // CP
        self.edge = self.spacing // 2
        self.tile = lax.axis_index("gy")
        self.upward = lax.rem(self.tile // 2, 2) == 0
        self.even = lax.rem(self.tile, 2) == 0
        self.sign = jnp.where(self.upward, 1, -1)

    def present(self, offset):
        there = (self.tile + offset >= 0) & (self.tile + offset < self.size)
        return select_flag(there)

    def share(self, row, point):
        start = (self.tile * self.rows).astype(jnp.float32)
        height = float(self.rows * self.size)
        place = jnp.clip(start + row + 0.5, 0.5 * self.spacing, height - 0.5 * self.spacing)
        centre = start + (point + 0.5) * self.spacing
        return jnp.maximum(0.0, 1.0 - jnp.abs(place - centre) / self.spacing)

    def edge_row(self, ahead, step):
        first, last = step, self.rows - 1 - step
        return jnp.where(self.upward == ahead, last, first)

    def side_point(self, ahead):
        return jnp.where(self.upward == ahead, jnp.float32(CP), jnp.float32(-1))

    def beside_term(self, row, ahead, rest_ref, small_ref):
        point = jnp.where(self.upward == ahead, CP - 1, 0)
        share = self.share(row, point.astype(jnp.float32))
        return share, rest_ref[point], small_ref[point, 0:1, 0:1], small_ref[point, 8:9, :]

    def side(self, left, ahead):
        sign = self.sign if ahead else -self.sign
        offsets = (sign, 2 * sign, 0 * sign)
        centre = (self.side_point(ahead) + 0.5) * self.spacing
        return self.point(left, centre, offsets)

    def point(self, left, centre, offsets):
        bases = [(offset * self.rows).astype(jnp.float32) for offset in offsets]
        return Point(left, centre, bases, [self.present(offset) for offset in offsets])


def mix_rows(mix_ref, terms, count):
    mixed = sum(share * rest.astype(jnp.float32) for share, rest, _, _ in terms)
    mix_ref[0:count, :] = mixed.astype(jnp.bfloat16)
    mix_ref[count:, :] = two_rows(sum(share * mean for share, _, _, mean in terms))
    return sum(share * diag for share, _, diag, _ in terms)


def write_mix(mix_ref, diag_ref, row, terms, count):
    diag_ref[row] = jnp.broadcast_to(mix_rows(mix_ref.at[row], terms, count), (8, 128))


def near_kernel(size, rows, has_far, *refs):
    own_ref, first_ref, other_ref = refs[:3]
    mix_ref, diag_ref, rest, small_ref, left, gram, square, last = refs[4 if has_far else 3 :]
    count, obs = own_ref.shape[0] - PAD, own_ref.shape[1]
    at = Place(size, rows)
    ahead_is_first = at.even == at.upward
    left[:, 0:obs] = jnp.where(ahead_is_first, first_ref[...], other_ref[...])
    left[:, obs : 2 * obs] = own_ref[...]
    left[:, 2 * obs : 3 * obs] = jnp.where(ahead_is_first, other_ref[...], first_ref[...])
    far = refs[3][...] if has_far else jnp.zeros(own_ref.shape, jnp.bfloat16)
    left[:, 3 * obs : 4 * obs] = far
    left[:, 4 * obs :] = own_ref[...]
    offsets = (at.sign, 0 * at.sign, -at.sign)
    points = []
    for point in range(CP):
        points.append(at.point(left.at[:, 0 : 3 * obs], (point + 0.5) * at.spacing, offsets))
    points.append(at.side(left.at[:, 2 * obs :], False))
    results = point_weights(points, count, float(rows), gram, square, last, rest)

    for point in range(CP):
        scalar_part, mean_weights = results[point]
        small_ref[point, 0:8, :] = jnp.broadcast_to(scalar_part, (8, count))
        small_ref[point, 8:16, :] = jnp.broadcast_to(mean_weights, (8, count))
    for row in range(at.edge, rows - at.edge):
        low = int((row + 0.5) / at.spacing - 0.5)
        terms = [
            (at.share(row, point), rest[point], *results[point]) for point in (low, low + 1)
        ]
        write_mix(mix_ref, diag_ref, row, terms, count)
    for step in range(at.edge):
        row = at.edge_row(False, step)
        terms = [
            at.beside_term(row, False, rest, small_ref),
            (at.share(row, at.side_point(False)), rest[CP], *results[CP]),
        ]
        write_mix(mix_ref, diag_ref, row, terms, count)


def weights(own, first, other, beyond, size, rows):
    count, obs = own.shape[0] - PAD, own.shape[1]
    near_inputs = [own, first, other] + ([] if beyond is None else [beyond])
    mix, diag, beside, small = pl.pallas_call(
        functools.partial(near_kernel, size, rows, beyond is not None),
        out_shape=(
            pltpu.VMEM((rows, count + PAD, count), jnp.bfloat16),
            pltpu.VMEM((rows, 8, 128), jnp.float32),
            pltpu.VMEM((CP + 1, count, count), jnp.bfloat16),
            pltpu.VMEM((CP, 16, count), jnp.float32),
        ),
        in_specs=[VMEM] * len(near_inputs),
        out_specs=(VMEM,) * 4,
        scratch_shapes=[pltpu.VMEM((count + PAD, 5 * obs), jnp.bfloat16)]
        + [pltpu.VMEM((CP + 1, count, count), jnp.bfloat16)] * 3,
        compiler_params=pltpu.CompilerParams(vmem_limit_bytes=40 * MIB),
        cost_estimate=pl.CostEstimate(
            flops=NEAR_FLOPS * count**3, bytes_accessed=8 * count * count, transcendentals=0
        ),
        name="near",
    )(*near_inputs)
    return mix, diag, beside, small


def finish_kernel(size, rows, *refs):
    own_ref, first_ref, other_ref, far_ref, mix_ref, diag_ref, beside_ref, small_ref = refs[:8]
    block_refs = refs[8:-9]
    out_ref, left, gram, square, last, rest, edge_mix, deviations, wide = refs[-9:]
    chips = len(block_refs)
    _, _, members, width = block_refs[0].shape
    count, obs = own_ref.shape[0] - PAD, own_ref.shape[1]
    at = Place(size, rows)
    chip = lax.axis_index("gx") // 2
    steps = exchange_steps(chips)
    halves = [(place, step, side) for place, step in enumerate(steps) for side in range(2)]

    def deviate(row):
        blocks = [block_refs[place][side, row].astype(jnp.float32) for place, _, side in halves]
        mean = sum(jnp.sum(block, axis=0, keepdims=True) for block in blocks) / count
        for (_, step, side), block in zip(halves, blocks):
            first = (2 * source_chip(chip, step, chips) + side) * members
            deviations[row, pl.ds(pl.multiple_of(first, members), members), :] = (
                block - mean
            ).astype(jnp.bfloat16)
        return mean

    def apply(row, mean, mix, diag):
        deviation = deviations[row]
        term = jnp.dot(mix, deviation, preferred_element_type=jnp.float32)
        shift = mean + term[count : count + 1] + term[count + 1 : count + 2]
        wide[pl.ds(row, count, stride=rows), :] = (
            term[0:count] + diag * deviation.astype(jnp.float32) + shift
        )

    def whole_row(row):
        apply(row, deviate(row), mix_ref[row], diag_ref[row, 0:1, 0:width])

    behind = [at.edge_row(False, step) for step in range(at.edge)]
    ahead = [at.edge_row(True, step) for step in range(at.edge)]
    means = []
    between = [functools.partial(whole_row, row) for row in range(at.edge, rows - at.edge)]
    between += [functools.partial(whole_row, row) for row in behind]
    between += [lambda: means.extend([deviate(row) for row in ahead])]

    left[:, 0:obs] = jnp.where(at.even == at.upward, first_ref[...], other_ref[...])
    left[:, obs : 2 * obs] = far_ref[...]
    left[:, 2 * obs :] = own_ref[...]
    points = [at.side(left, True)]
    results = point_weights(points, count, float(rows), gram, square, last, rest, between)
    for step, row in enumerate(ahead):
        terms = [
            (at.share(row, at.side_point(True)), rest[0], *results[0]),
            at.beside_term(row, True, beside_ref, small_ref),
        ]
        diag = mix_rows(edge_mix.at[step], terms, count)
        apply(row, means[step], edge_mix[step], diag)
    out_ref[...] = wide[...].astype(jnp.bfloat16)


def finish(tiles, mixes, blocks, size):
    _, rows, members, width = blocks[0].shape
    count, obs = tiles[0].shape[0] - PAD, tiles[0].shape[1]
    square = pltpu.VMEM((1, count, count), jnp.bfloat16)
    flat = pl.pallas_call(
        functools.partial(finish_kernel, size, rows),
        out_shape=jax.ShapeDtypeStruct((count * rows, width), jnp.bfloat16),
        in_specs=[VMEM] * (8 + len(blocks)),
        out_specs=VMEM,
        scratch_shapes=[
            pltpu.VMEM((count + PAD, 3 * obs), jnp.bfloat16),
            square,
            square,
            square,
            square,
            pltpu.VMEM((rows // CP // 2, count + PAD, count), jnp.bfloat16),
            pltpu.VMEM((rows, count, width), jnp.bfloat16),
            pltpu.VMEM((count * rows, width), jnp.float32),
        ],
        compiler_params=pltpu.CompilerParams(vmem_limit_bytes=40 * MIB),
        name="finish",
    )(*tiles, *mixes, *blocks)
    return flat.reshape(count, rows, width)


def on_device(prior_fields, measured_spread, scaled_misfit, sensor_line_inside):
    parts = lax.axis_size("gx")
    chips = parts // 2
    size = lax.axis_size("gy")
    count = measured_spread.shape[0]
    rows = prior_fields.shape[1]
    packed, keep, give = split(
        prior_fields,
        measured_spread.reshape(count, -1),
        scaled_misfit.reshape(1, -1),
        sensor_line_inside.reshape(1, -1),
        chips,
    )

    def trade(pairs):
        if not pairs:
            return None
        return lax.ppermute(packed, ("gx", "gy"), everyone(pairs, parts, size))

    got = lax.ppermute(give, "gx", [(index, index ^ 1) for index in range(parts)])
    first = trade(swap_pairs(size, 1, 0))
    other = trade(swap_pairs(size, 1, 1))
    far, beyond = trade(swap_pairs(size, 2, 0)), trade(swap_pairs(size, 2, 1))
    own_blocks = sort(keep, got)
    blocks = [own_blocks[0]]
    for step in exchange_steps(chips)[1:]:
        pairs = [
            (index, 2 * target_chip(index // 2, step, chips) + index % 2) for index in range(parts)
        ]
        blocks.append(lax.ppermute(own_blocks[step], "gx", pairs))
    mixes = weights(packed, first, other, beyond, size, rows)
    return finish((packed, first, other, far), mixes, blocks, size)


def solution(mesh):
    return jax.shard_map(
        on_device,
        mesh=mesh,
        in_specs=(P("gx", "gy", None), P(None, "gy", "gx"), P("gy", "gx"), P("gy", "gx")),
        out_specs=P(None, "gy", "gx"),
        check_vma=False,
    )
```

```python
import functools

import jax
import jax.numpy as jnp
from jax import lax
from jax.experimental import pallas as pl
from jax.experimental.pallas import tpu as pltpu
from jax.sharding import PartitionSpec as P

CP = 2
PAD = 16
MIB = 1 << 20
NEAR_FLOPS = 180

VMEM = pl.BlockSpec(memory_space=pltpu.VMEM)
HBM = pl.BlockSpec(memory_space=pltpu.HBM)


def swap_pairs(size, reach, phase):
    lows = [i for i in range(size - reach) if (i // reach) % 2 == phase]
    return [pair for i in lows for pair in ((i, i + reach), (i + reach, i))]


def everyone(pairs, parts, size):
    idle = set(range(size)) - {place for pair in pairs for place in pair}
    moves = [(c * size + i, c * size + j) for c in range(parts) for i, j in pairs]
    return moves + [(c * size + i, (c ^ 1) * size + i) for c in range(parts) for i in sorted(idle)]


def target_chip(chip, step, chips):
    if chips & (chips - 1) == 0:
        return chip ^ step
    return (chip + step) % chips if isinstance(chip, int) else lax.rem(chip + step, chips)


def exchange_steps(chips):
    return [0] + sorted(range(1, chips), key=lambda step: -step.bit_count())


def source_chip(chip, step, chips):
    return target_chip(chip, step if chips & (chips - 1) == 0 else chips - step, chips)


def split_kernel(chips, prior_ref, spread_ref, misfit_ref, line_ref, *refs):
    packed_ref, keep_ref, give_ref, misfit, line, sems = refs
    count, width = spread_ref.shape
    copies = [
        pltpu.make_async_copy(spread_ref, packed_ref.at[0:count], sems.at[0]),
        pltpu.make_async_copy(misfit_ref, misfit, sems.at[1]),
        pltpu.make_async_copy(line_ref, line, sems.at[2]),
    ]
    core = lax.rem(lax.axis_index("gx"), 2)
    cells = prior_ref.shape[2] // (2 * chips)
    for chip in range(chips):
        for place, (side, ref) in enumerate(((core, keep_ref), (1 - core, give_ref))):
            first = pl.multiple_of((2 * chip + side) * cells, cells)
            copies.append(
                pltpu.make_async_copy(
                    prior_ref.at[:, :, pl.ds(first, cells)],
                    ref.at[chip],
                    sems.at[3 + 2 * chip + place],
                )
            )
    for copy in copies:
        copy.start()
    for copy in copies[1:3]:
        copy.wait()
    which = lax.broadcasted_iota(jnp.int32, (PAD, width), 0)
    misfits = jnp.broadcast_to(misfit[...].astype(jnp.float32), (PAD, width))
    lines = jnp.broadcast_to(line[...].astype(jnp.float32), (PAD, width))
    extra = jnp.where(which == 0, misfits, jnp.where(which == 1, lines, 0.0))
    packed_ref[count:, :] = extra.astype(jnp.bfloat16)
    copies[0].wait()
    for copy in copies[3:]:
        copy.wait()


def split(prior, spread, misfit, line, chips):
    members, rows, cells = prior.shape
    count, obs = spread.shape
    half = (chips, members, rows, cells // (2 * chips))
    inputs = (prior, spread, misfit, line)
    return pl.pallas_call(
        functools.partial(split_kernel, chips),
        out_shape=(
            pltpu.VMEM((count + PAD, obs), jnp.bfloat16),
            pltpu.VMEM(half, jnp.bfloat16),
            pltpu.VMEM(half, jnp.bfloat16),
        ),
        in_specs=[HBM] * 4,
        out_specs=(VMEM,) * 3,
        scratch_shapes=[
            pltpu.VMEM(misfit.shape, misfit.dtype),
            pltpu.VMEM(line.shape, line.dtype),
            pltpu.SemaphoreType.DMA((3 + 2 * chips,)),
        ],
        name="split",
    )(*[pltpu.with_memory_space_constraint(array, pltpu.HBM) for array in inputs])


def sort_kernel(chips, rows, keep_ref, got_ref, *refs):
    sorted_refs, wide = refs[:chips], refs[chips]
    members = keep_ref.shape[0] // (chips * rows)
    index = lax.axis_index("gx")
    core = lax.rem(index, 2)
    chip = index // 2
    for half, ref in enumerate((keep_ref, got_ref)):
        wide[half] = ref[...].astype(jnp.float32)
    for step in range(chips):
        first = target_chip(chip, step, chips) * (members * rows)
        for half, side in enumerate((core, 1 - core)):
            for row in range(rows):
                lines = wide[half, pl.ds(first + row, members, stride=rows), :]
                sorted_refs[step][side, row] = lines.astype(jnp.bfloat16)


def sort(keep, got):
    chips, members, rows, cells = keep.shape
    flat = (chips * members * rows, cells)
    return pl.pallas_call(
        functools.partial(sort_kernel, chips, rows),
        out_shape=[pltpu.VMEM((2, rows, members, cells), jnp.bfloat16)] * chips,
        in_specs=[VMEM] * 2,
        out_specs=[VMEM] * chips,
        scratch_shapes=[pltpu.VMEM((2,) + flat, jnp.float32)],
        compiler_params=pltpu.CompilerParams(vmem_limit_bytes=16 * MIB),
        cost_estimate=pl.CostEstimate(flops=0, bytes_accessed=4 * MIB, transcendentals=0),
        name="sort",
    )(keep.reshape(flat), got.reshape(flat))


def select_flag(condition):
    return jnp.where(condition, jnp.float32(1.0), jnp.float32(0.0))


class Point:
    def __init__(self, left, centre, bases, present):
        self.left, self.centre, self.bases, self.present = left, centre, bases, present


def turn(row, eye):
    block = eye.shape[0]
    pieces = [row[:, i : i + block] for i in range(0, row.shape[1], block)]
    return jnp.concatenate(
        [jnp.sum(eye * piece, axis=1, keepdims=True) for piece in pieces], axis=0
    )


def lay(column, eye):
    block = eye.shape[0]
    pieces = [column[i : i + block] for i in range(0, column.shape[0], block)]
    return jnp.concatenate(
        [jnp.sum(eye * piece, axis=0, keepdims=True) for piece in pieces], axis=1
    )


def point_weights(points, count, radius, gram_ref, square_ref, last_ref, rest_ref, between=()):
    pieces = iter(between)
    share = 1.0 / (count - 1.0)
    slots = range(len(points))
    block = min(count, 128)
    eye = jnp.where(
        lax.broadcasted_iota(jnp.int32, (block, block), 0)
        == lax.broadcasted_iota(jnp.int32, (block, block), 1),
        1.0,
        0.0,
    )
    drives, bounds = [], []
    for slot in slots:
        point = points[slot]
        left = point.left
        line = left[count + 1 : count + 2, :].astype(jnp.float32)
        obs = line.shape[1] // 3
        where = lax.broadcasted_iota(jnp.int32, line.shape, 1) // obs
        first, second, third = point.bases
        base = jnp.where(where == 0, first, jnp.where(where == 1, second, third))
        first, second, third = point.present
        alive = jnp.where(where == 0, first, jnp.where(where == 1, second, third))
        distance = (base + line + 0.5 - point.centre) / radius
        locality = jnp.exp(-0.5 * distance * distance) * alive
        scaled = (left[0:count, :].astype(jnp.float32) * locality).astype(jnp.bfloat16)
        both = lax.dot_general(
            left[...], scaled, (((1,), (1,)), ((), ())), preferred_element_type=jnp.float32
        )
        gram = both[0:count]
        drives.append(both[count : count + 1])
        gram_ref[slot] = gram.astype(jnp.bfloat16)
        sizes = jnp.sum(jnp.abs(gram), axis=0, keepdims=True)
        bounds.append(1.0 + share * jnp.max(sizes, axis=1, keepdims=True))
    next(pieces, int)()
    factors = []
    for slot in slots:
        s = 1.0 / bounds[slot]
        g = s * share
        root = lax.rsqrt(bounds[slot])
        wide = lambda value: jnp.broadcast_to(value, (1, count))
        third = wide((4.0 * s - 9.0) * (g * g) * g * (root / 16.0))
        fourth = wide((g * g) * (g * g) * (root / 16.0))
        linear = wide((-39.0 + s * (54.0 + s * (-27.0 + 4.0 * s))) * g * (root / 16.0))
        quadratic = wide((27.0 + s * (-27.0 + 6.0 * s)) * (g * g) * (root / 16.0))
        scalar_part = (36.0 + s * (-39.0 + s * (27.0 + s * (-9.0 + s)))) * (root / 16.0)
        factors.append((linear, quadratic, scalar_part, g * bounds[slot]))
        gram = gram_ref[slot]
        square = jnp.dot(gram, gram, preferred_element_type=jnp.float32)
        square_ref[slot] = square.astype(jnp.bfloat16)
        last = third * gram.astype(jnp.float32) + fourth * square
        last_ref[slot] = last.astype(jnp.bfloat16)
    next(pieces, int)()
    for slot in slots:
        linear, quadratic, scalar_part, _ = factors[slot]
        product = jnp.dot(square_ref[slot], last_ref[slot], preferred_element_type=jnp.float32)
        rest = (
            linear * gram_ref[slot].astype(jnp.float32)
            + quadratic * square_ref[slot].astype(jnp.float32)
            + product
        )
        rest_ref[slot] = rest.astype(jnp.bfloat16)

    next(pieces, int)()
    results = []
    for slot in slots:
        _, _, scalar_part, g = factors[slot]
        mean_weights = drives[slot]
        for _ in range(2):
            out = jnp.dot(two_rows(mean_weights), rest_ref[slot], preferred_element_type=jnp.float32)
            mean_weights = out[0:1] + out[1:2] + scalar_part * mean_weights
            next(pieces, int)()
        mean_weights = mean_weights * g
        results.append((scalar_part, mean_weights))
    return results


def two_rows(row):
    high = row.astype(jnp.bfloat16).astype(jnp.float32)
    which = lax.broadcasted_iota(jnp.int32, (PAD, row.shape[1]), 0)
    return jnp.where(which == 0, high, jnp.where(which == 1, row - high, 0.0)).astype(jnp.bfloat16)


class Place:
    def __init__(self, size, rows):
        self.size, self.rows = size, rows
        self.spacing = rows // CP
        self.edge = self.spacing // 2
        self.tile = lax.axis_index("gy")
        self.upward = lax.rem(self.tile // 2, 2) == 0
        self.even = lax.rem(self.tile, 2) == 0
        self.sign = jnp.where(self.upward, 1, -1)

    def present(self, offset):
        there = (self.tile + offset >= 0) & (self.tile + offset < self.size)
        return select_flag(there)

    def share(self, row, point):
        start = (self.tile * self.rows).astype(jnp.float32)
        height = float(self.rows * self.size)
        place = jnp.clip(start + row + 0.5, 0.5 * self.spacing, height - 0.5 * self.spacing)
        centre = start + (point + 0.5) * self.spacing
        return jnp.maximum(0.0, 1.0 - jnp.abs(place - centre) / self.spacing)

    def edge_row(self, ahead, step):
        first, last = step, self.rows - 1 - step
        return jnp.where(self.upward == ahead, last, first)

    def side_point(self, ahead):
        return jnp.where(self.upward == ahead, jnp.float32(CP), jnp.float32(-1))

    def beside_term(self, row, ahead, rest_ref, small_ref):
        point = jnp.where(self.upward == ahead, CP - 1, 0)
        share = self.share(row, point.astype(jnp.float32))
        return share, rest_ref[point], small_ref[point, 0:1, 0:1], small_ref[point, 8:9, :]

    def side(self, left, ahead):
        sign = self.sign if ahead else -self.sign
        offsets = (sign, 2 * sign, 0 * sign)
        centre = (self.side_point(ahead) + 0.5) * self.spacing
        return self.point(left, centre, offsets)

    def point(self, left, centre, offsets):
        bases = [(offset * self.rows).astype(jnp.float32) for offset in offsets]
        return Point(left, centre, bases, [self.present(offset) for offset in offsets])


def mix_rows(mix_ref, terms, count):
    mixed = sum(share * rest.astype(jnp.float32) for share, rest, _, _ in terms)
    mix_ref[0:count, :] = mixed.astype(jnp.bfloat16)
    mix_ref[count:, :] = two_rows(sum(share * mean for share, _, _, mean in terms))
    return sum(share * diag for share, _, diag, _ in terms)


def write_mix(mix_ref, diag_ref, row, terms, count):
    diag_ref[row] = jnp.broadcast_to(mix_rows(mix_ref.at[row], terms, count), (8, 128))


def near_kernel(size, rows, has_far, *refs):
    own_ref, first_ref, other_ref = refs[:3]
    mix_ref, diag_ref, rest, small_ref, left, gram, square, last = refs[4 if has_far else 3 :]
    count, obs = own_ref.shape[0] - PAD, own_ref.shape[1]
    at = Place(size, rows)
    ahead_is_first = at.even == at.upward
    left[:, 0:obs] = jnp.where(ahead_is_first, first_ref[...], other_ref[...])
    left[:, obs : 2 * obs] = own_ref[...]
    left[:, 2 * obs : 3 * obs] = jnp.where(ahead_is_first, other_ref[...], first_ref[...])
    far = refs[3][...] if has_far else jnp.zeros(own_ref.shape, jnp.bfloat16)
    left[:, 3 * obs : 4 * obs] = far
    left[:, 4 * obs :] = own_ref[...]
    offsets = (at.sign, 0 * at.sign, -at.sign)
    points = []
    for point in range(CP):
        points.append(at.point(left.at[:, 0 : 3 * obs], (point + 0.5) * at.spacing, offsets))
    points.append(at.side(left.at[:, 2 * obs :], False))
    results = point_weights(points, count, float(rows), gram, square, last, rest)

    for point in range(CP):
        scalar_part, mean_weights = results[point]
        small_ref[point, 0:8, :] = jnp.broadcast_to(scalar_part, (8, count))
        small_ref[point, 8:16, :] = jnp.broadcast_to(mean_weights, (8, count))
    for row in range(at.edge, rows - at.edge):
        low = int((row + 0.5) / at.spacing - 0.5)
        terms = [
            (at.share(row, point), rest[point], *results[point]) for point in (low, low + 1)
        ]
        write_mix(mix_ref, diag_ref, row, terms, count)
    for step in range(at.edge):
        row = at.edge_row(False, step)
        terms = [
            at.beside_term(row, False, rest, small_ref),
            (at.share(row, at.side_point(False)), rest[CP], *results[CP]),
        ]
        write_mix(mix_ref, diag_ref, row, terms, count)


def weights(own, first, other, beyond, size, rows):
    count, obs = own.shape[0] - PAD, own.shape[1]
    near_inputs = [own, first, other] + ([] if beyond is None else [beyond])
    mix, diag, beside, small = pl.pallas_call(
        functools.partial(near_kernel, size, rows, beyond is not None),
        out_shape=(
            pltpu.VMEM((rows, count + PAD, count), jnp.bfloat16),
            pltpu.VMEM((rows, 8, 128), jnp.float32),
            pltpu.VMEM((CP + 1, count, count), jnp.bfloat16),
            pltpu.VMEM((CP, 16, count), jnp.float32),
        ),
        in_specs=[VMEM] * len(near_inputs),
        out_specs=(VMEM,) * 4,
        scratch_shapes=[pltpu.VMEM((count + PAD, 5 * obs), jnp.bfloat16)]
        + [pltpu.VMEM((CP + 1, count, count), jnp.bfloat16)] * 3,
        compiler_params=pltpu.CompilerParams(vmem_limit_bytes=40 * MIB),
        cost_estimate=pl.CostEstimate(
            flops=NEAR_FLOPS * count**3, bytes_accessed=8 * count * count, transcendentals=0
        ),
        name="near",
    )(*near_inputs)
    return mix, diag, beside, small


def finish_kernel(size, rows, *refs):
    own_ref, first_ref, other_ref, far_ref, mix_ref, diag_ref, beside_ref, small_ref = refs[:8]
    block_refs = refs[8:-9]
    out_ref, left, gram, square, last, rest, edge_mix, deviations, wide = refs[-9:]
    chips = len(block_refs)
    _, _, members, width = block_refs[0].shape
    count, obs = own_ref.shape[0] - PAD, own_ref.shape[1]
    at = Place(size, rows)
    chip = lax.axis_index("gx") // 2
    steps = exchange_steps(chips)
    halves = [(place, step, side) for place, step in enumerate(steps) for side in range(2)]

    def deviate(row):
        blocks = [block_refs[place][side, row].astype(jnp.float32) for place, _, side in halves]
        mean = sum(jnp.sum(block, axis=0, keepdims=True) for block in blocks) / count
        for (_, step, side), block in zip(halves, blocks):
            first = (2 * source_chip(chip, step, chips) + side) * members
            deviations[row, pl.ds(pl.multiple_of(first, members), members), :] = (
                block - mean
            ).astype(jnp.bfloat16)
        return mean

    def apply(row, mean, mix, diag):
        deviation = deviations[row]
        term = jnp.dot(mix, deviation, preferred_element_type=jnp.float32)
        shift = mean + term[count : count + 1] + term[count + 1 : count + 2]
        wide[pl.ds(row, count, stride=rows), :] = (
            term[0:count] + diag * deviation.astype(jnp.float32) + shift
        )

    def whole_row(row):
        apply(row, deviate(row), mix_ref[row], diag_ref[row, 0:1, 0:width])

    behind = [at.edge_row(False, step) for step in range(at.edge)]
    ahead = [at.edge_row(True, step) for step in range(at.edge)]
    means = []
    near_rows = list(range(at.edge, rows - at.edge)) + behind
    near_means = [deviate(row) for row in near_rows]
    means.extend([deviate(row) for row in ahead])

    def near_row(place):
        row = near_rows[place]
        apply(row, near_means[place], mix_ref[row], diag_ref[row, 0:1, 0:width])

    between = [functools.partial(near_row, place) for place in range(len(near_rows))]

    left[:, 0:obs] = jnp.where(at.even == at.upward, first_ref[...], other_ref[...])
    left[:, obs : 2 * obs] = far_ref[...]
    left[:, 2 * obs :] = own_ref[...]
    points = [at.side(left, True)]
    results = point_weights(points, count, float(rows), gram, square, last, rest, between)
    for step, row in enumerate(ahead):
        terms = [
            (at.share(row, at.side_point(True)), rest[0], *results[0]),
            at.beside_term(row, True, beside_ref, small_ref),
        ]
        diag = mix_rows(edge_mix.at[step], terms, count)
        apply(row, means[step], edge_mix[step], diag)
    quarter = count * rows // 4
    for part in range(4):
        lines = pl.ds(part * quarter, quarter)
        out_ref[lines, :] = wide[lines, :].astype(jnp.bfloat16)


def finish(tiles, mixes, blocks, size):
    _, rows, members, width = blocks[0].shape
    count, obs = tiles[0].shape[0] - PAD, tiles[0].shape[1]
    square = pltpu.VMEM((1, count, count), jnp.bfloat16)
    flat = pl.pallas_call(
        functools.partial(finish_kernel, size, rows),
        out_shape=jax.ShapeDtypeStruct((count * rows, width), jnp.bfloat16),
        in_specs=[VMEM] * (8 + len(blocks)),
        out_specs=VMEM,
        scratch_shapes=[
            pltpu.VMEM((count + PAD, 3 * obs), jnp.bfloat16),
            square,
            square,
            square,
            square,
            pltpu.VMEM((rows // CP // 2, count + PAD, count), jnp.bfloat16),
            pltpu.VMEM((rows, count, width), jnp.bfloat16),
            pltpu.VMEM((count * rows, width), jnp.float32),
        ],
        compiler_params=pltpu.CompilerParams(vmem_limit_bytes=40 * MIB),
        name="finish",
    )(*tiles, *mixes, *blocks)
    return flat.reshape(count, rows, width)


def on_device(prior_fields, measured_spread, scaled_misfit, sensor_line_inside):
    parts = lax.axis_size("gx")
    chips = parts // 2
    size = lax.axis_size("gy")
    count = measured_spread.shape[0]
    rows = prior_fields.shape[1]
    packed, keep, give = split(
        prior_fields,
        measured_spread.reshape(count, -1),
        scaled_misfit.reshape(1, -1),
        sensor_line_inside.reshape(1, -1),
        chips,
    )

    def trade(pairs):
        if not pairs:
            return None
        return lax.ppermute(packed, ("gx", "gy"), everyone(pairs, parts, size))

    got = lax.ppermute(give, "gx", [(index, index ^ 1) for index in range(parts)])
    first = trade(swap_pairs(size, 1, 0))
    other = trade(swap_pairs(size, 1, 1))
    far, beyond = trade(swap_pairs(size, 2, 0)), trade(swap_pairs(size, 2, 1))
    own_blocks = sort(keep, got)
    blocks = [own_blocks[0]]
    for step in exchange_steps(chips)[1:]:
        pairs = [
            (index, 2 * target_chip(index // 2, step, chips) + index % 2) for index in range(parts)
        ]
        blocks.append(lax.ppermute(own_blocks[step], "gx", pairs))
    mixes = weights(packed, first, other, beyond, size, rows)
    return finish((packed, first, other, far), mixes, blocks, size)


def solution(mesh):
    return jax.shard_map(
        on_device,
        mesh=mesh,
        in_specs=(P("gx", "gy", None), P(None, "gy", "gx"), P("gy", "gx"), P("gy", "gx")),
        out_specs=P(None, "gy", "gx"),
        check_vma=False,
    )
```
